32 devices in a mesh: groups: 2 (over x), gx: 8 (over z, y), gy: 2 (over core).
Axes of the slice: x: 2, y: 2, z: 4, core: 2. Of those that a mesh axis runs over, the one named last changes fastest.
Arguments:
- level_set: float32 [1024, 128, 128], P(('groups', 'gx'), 'gy'), parts along dimension 0, may hold values from -115 to 115
- band: int32 [32, 4, 4], P('groups'), parts along dimension 0, may hold values 0 or 1
Outputs:
- normals: float32 [3, 1024, 128, 128], P(None, ('groups', 'gx'), 'gy'), parts along dimension 1
- curvature: float32 [1024, 128, 128], P(('groups', 'gx'), 'gy'), parts along dimension 0
The draws below stay inside these ranges and needn't reach their ends.
There are 2 independent parts, one for each index of `groups`. The reference program is written for one: setup_inputs(seed, part) draws one part's arguments, and reference() takes and returns one part's arrays. A program takes and returns all parts, laid end to end along the dimension named above; each array names one. Nothing has to cross between parts.
All inputs are finite; a program needn't handle non-finite values.
Results may differ from the reference program's by a relative error of at most 0.00019.
Values sent between devices are 32-bit elements; how exact they have to be, the bound alone decides.
A program may use at most 128 MiB of HBM per device.

```python
import math
import jax
import jax.numpy as jnp
from jax import lax

NZ = 128
HALF_TAPS = 20
BLOCK = 32
NX = 512
NY = 128


def draw_level_set(key, part):
    key = jax.random.fold_in(key, 17)
    streams = jax.random.split(key, 5)
    count = 16
    cos_polar = jax.random.uniform(streams[0], (count,), jnp.float32, -1.0, 1.0)
    azimuth = jax.random.uniform(streams[1], (count,), jnp.float32, -math.pi, math.pi)
    sin_polar = jnp.sqrt(1.0 - cos_polar * cos_polar)
    wavelength = jnp.exp(jax.random.uniform(streams[2], (count,), jnp.float32, math.log(20.0), math.log(60.0)))
    wavenumber = 2.0 * math.pi / wavelength
    phase = jax.random.uniform(streams[3], (count,), jnp.float32, -math.pi, math.pi)
    amplitude = 0.7 / wavenumber
    coord_x = jnp.arange(NX).astype(jnp.float32)[:, None, None]
    coord_y = jnp.arange(NY).astype(jnp.float32)[None, :, None]
    coord_z = jnp.arange(NZ).astype(jnp.float32)[None, None, :]
    summed = jnp.zeros((NX, NY, NZ), jnp.float32)
    for index in range(count):
        along = sin_polar[index] * jnp.cos(azimuth[index]) * coord_x
        along = along + sin_polar[index] * jnp.sin(azimuth[index]) * coord_y
        along = along + cos_polar[index] * coord_z
        summed = summed + amplitude[index] * jnp.sin(wavenumber[index] * along + phase[index])
    rough = 0.3 * jax.random.truncated_normal(streams[4], -3.0, 3.0, (NX, NY, NZ), jnp.float32)
    summed = summed + rough
    return summed


def with_ends(drawn, rng, least, high):
    place = [jax.random.randint(jax.random.fold_in(rng, axis), (), 0, length) for axis, length in enumerate(drawn.shape)]
    longest = drawn.shape.index(max(drawn.shape))
    beside = place[:longest] + [(place[longest] + 1) % drawn.shape[longest]] + place[longest + 1:]
    return drawn.at[tuple(place)].set(least).at[tuple(beside)].set(high)


def setup_inputs(seed: int = 0, part: int = 0) -> dict:
    key_list = jax.random.split(jax.random.key(seed), 3)
    own_keys = jax.random.split(jax.random.fold_in(key_list[2], part), 3)
    return {
        "level_set": draw_level_set(jax.random.fold_in(jax.random.fold_in(key_list[2], part), 71), part),
        "band": with_ends((jax.random.randint(own_keys[1], (NX // BLOCK, NY // BLOCK, NZ // BLOCK), 0, 3) < 1).astype(jnp.int32), jax.random.fold_in(own_keys[1], 1), 0, 1),
    }


SIGMA_CELLS = 7.0
FLOOR_SQ = 0.05

def make_filters():
    offsets = jnp.arange(-HALF_TAPS, HALF_TAPS + 1).astype(jnp.float32)
    bell_curve = jnp.exp(-offsets * offsets / (2.0 * SIGMA_CELLS * SIGMA_CELLS))
    smooth_taps = bell_curve / jnp.sum(bell_curve)
    slope_taps = offsets * smooth_taps / jnp.sum(offsets * offsets * smooth_taps)
    return (smooth_taps, slope_taps)

def filter_valid(padded, weights, axis_pos, length):
    summed = weights[0] * lax.slice_in_dim(padded, 0, length, axis=axis_pos)
    for offset in range(1, 2 * HALF_TAPS + 1):
        summed = summed + weights[offset] * lax.slice_in_dim(padded, offset, offset + length, axis=axis_pos)
    return summed

def filter_full(values_in, weights, axis_pos):
    widths = [(0, 0)] * values_in.ndim
    widths[axis_pos] = (HALF_TAPS, HALF_TAPS)
    return filter_valid(jnp.pad(values_in, widths), weights, axis_pos, values_in.shape[axis_pos])

def fourth_diff(padded, axis_pos, length):
    first = lax.slice_in_dim(padded, 0, length, axis=axis_pos)
    second = lax.slice_in_dim(padded, 1, length + 1, axis=axis_pos)
    fourth = lax.slice_in_dim(padded, 3, length + 3, axis=axis_pos)
    fifth = lax.slice_in_dim(padded, 4, length + 4, axis=axis_pos)
    return (first - 8.0 * second + 8.0 * fourth - fifth) / 12.0

def reference(level_set, band):
    smooth_taps, slope_taps = make_filters()
    z_smooth = filter_full(level_set, smooth_taps, 2)
    z_slope = filter_full(level_set, slope_taps, 2)
    both_smooth = filter_full(z_smooth, smooth_taps, 1)
    y_slope = filter_full(z_smooth, slope_taps, 1)
    z_only = filter_full(z_slope, smooth_taps, 1)
    grad_x = filter_full(both_smooth, slope_taps, 0)
    grad_y = filter_full(y_slope, smooth_taps, 0)
    grad_z = filter_full(z_only, smooth_taps, 0)
    square = grad_x * grad_x + grad_y * grad_y + grad_z * grad_z
    inverse = lax.rsqrt(jnp.maximum(square, FLOOR_SQ))
    normals = jnp.stack([grad_x * inverse, grad_y * inverse, grad_z * inverse])
    padded = jnp.pad(normals, ((0, 0), (2, 2), (2, 2), (2, 2)))
    divergence = fourth_diff(padded[0][:, 2:-2, 2:-2], 0, NX)
    divergence = divergence + fourth_diff(padded[1][2:-2, :, 2:-2], 1, NY)
    divergence = divergence + fourth_diff(padded[2][2:-2, 2:-2, :], 2, NZ)
    cells = band.astype(jnp.float32)
    cells = jnp.repeat(jnp.repeat(jnp.repeat(cells, BLOCK, axis=0), BLOCK, axis=1), BLOCK, axis=2)
    return (normals, divergence * cells)
```

```python
import functools

import jax
import jax.numpy as jnp
from jax import lax
from jax.experimental import pallas as pl
from jax.experimental.pallas import tpu as pltpu
from jax.sharding import PartitionSpec as P

HALF_TAPS = 20
BLOCK = 32
SIGMA_CELLS = 7.0
FLOOR_SQ = 0.05
RIM = 2
REACH = HALF_TAPS + RIM
SIDE = 24
YPAD = 96
YOUT = 80


def weights(source, target, valid):
    offsets = jnp.arange(-HALF_TAPS, HALF_TAPS + 1).astype(jnp.float32)
    bell = jnp.exp(-offsets * offsets / (2.0 * SIGMA_CELLS * SIGMA_CELLS))
    total = jnp.sum(bell)
    moment = jnp.sum(offsets * offsets * (bell / total))
    distance = (source[None, :] - target[:, None]).astype(jnp.float32)
    values = jnp.exp(-distance * distance / (2.0 * SIGMA_CELLS * SIGMA_CELLS)) / total
    values = jnp.where((jnp.abs(distance) <= HALF_TAPS) & valid, values, 0.0)
    return values, distance * values / moment


def halves(values):
    high = values.astype(jnp.bfloat16)
    low = (values - high.astype(jnp.float32)).astype(jnp.bfloat16)
    return high, low


def weight_halves(values):
    high = lax.reduce_precision(values, 8, 7)
    return high.astype(jnp.bfloat16), (values - high).astype(jnp.bfloat16)


def left_matrix(values):
    high, low = weight_halves(values)
    return jnp.concatenate([high, high, low], axis=1)


def stack_halves(values):
    high, low = halves(values)
    return jnp.concatenate([high, low, high], axis=0)


def dot(a, b):
    return jnp.dot(a, b, preferred_element_type=jnp.float32)


def filter_rows(src, rows, out_rows, zmat, xmat, ymat, mid, emit):
    width = 64 + SIDE
    for c in range(3):
        for x in range(out_rows):
            mid[c, pl.ds(x * YPAD + width, YPAD - width), :] = jnp.zeros((YPAD - width, 128), jnp.float32)

    def columns(group, carry):
        lines = [src[pl.ds(group * 8 + i, rows, stride=width), :] for i in range(8)]
        high, low = halves(jnp.concatenate(lines, axis=0))
        along_z = dot(jnp.concatenate([high, low, high], axis=1), zmat[...])
        high, low = halves(along_z)
        for i in range(8):
            part = slice(i * rows, (i + 1) * rows)
            both = dot(xmat[...], jnp.concatenate([high[part], low[part], high[part]], axis=0))
            place = pl.ds(group * 8 + i, out_rows, stride=YPAD)
            mid[0, place, :] = both[:out_rows, :128]
            mid[1, place, :] = both[out_rows:, :128]
            mid[2, place, :] = both[out_rows:, 128:]
        return carry

    lax.fori_loop(0, width // 8, columns, 0)

    def planes(x, carry):
        place = pl.ds(pl.multiple_of(x * YPAD, 8), YPAD)
        first = stack_halves(mid[0, place, :])
        second = stack_halves(mid[1, place, :])
        third = stack_halves(mid[2, place, :])
        ends = dot(ymat[:YOUT, :], jnp.concatenate([first, third], axis=1))
        emit(x, ends[:, :128], dot(ymat[YOUT:, :], second), ends[:, 128:])
        return carry

    lax.fori_loop(0, out_rows, planes, 0, unroll=4)


def local_kernel(rows, out_rows, own, peer, zmat, xmat, ymat, grad, src, mid, sems):
    width = 64 + SIDE
    copies = []
    for x in range(rows):
        copies.append(pltpu.make_async_copy(own.at[x], src.at[pl.ds(x * width, 64)], sems.at[0]))
        copies.append(pltpu.make_async_copy(peer.at[x], src.at[pl.ds(x * width + 64, SIDE)], sems.at[1]))
    for copy in copies:
        copy.start()
    for copy in copies:
        copy.wait()

    def emit(x, first, second, third):
        grad[0, x] = first
        grad[1, x] = second
        grad[2, x] = third

    filter_rows(src, rows, out_rows, zmat, xmat, ymat, mid, emit)


def edge_kernel(
    rows, low, high, low_peer, high_peer, grad_in, cells, zmat, xmat, ymat, normals, curvature,
    src, mid, grad, curv, sems, out_sems
):
    width = 64 + SIDE
    load = pltpu.make_async_copy(grad_in, grad, sems.at[4])
    load.start()
    copies = []
    for x in range(REACH):
        for number, (ref, base, col, count) in enumerate(
            ((low, 0, 0, 64), (high, SIDE, 0, 64), (low_peer, 0, 64, SIDE), (high_peer, SIDE, 64, SIDE))
        ):
            place = pl.ds((base + x) * width + col, count)
            copies.append(pltpu.make_async_copy(ref.at[x], src.at[place], sems.at[number]))
    for copy in copies:
        copy.start()
    for base in (REACH, SIDE + REACH):
        src[pl.ds(base * width, (SIDE - REACH) * width), :] = jnp.zeros(((SIDE - REACH) * width, 128), jnp.float32)
    for copy in copies:
        copy.wait()
    load.wait()

    shift = rows + 2 * RIM - 2 * SIDE

    def emit(x, first, second, third):
        target = x + jnp.where(x < SIDE, 0, shift)
        grad[0, target] = grad[0, target] + first
        grad[1, target] = grad[1, target] + second
        grad[2, target] = grad[2, target] + third

    filter_rows(src, 2 * SIDE, 2 * SIDE, zmat, xmat, ymat, mid, emit)

    def unit(x):
        first, second, third = grad[0, x], grad[1, x], grad[2, x]
        inverse = lax.rsqrt(jnp.maximum(first * first + second * second + third * third, FLOOR_SQ))
        grad[0, x] = first * inverse
        grad[1, x] = second * inverse
        grad[2, x] = third * inverse

    for x in range(2 * RIM):
        unit(x)
    lane = lax.broadcasted_iota(jnp.int32, (64, 128), 1)

    def plane(x, carry):
        unit(x + 2 * RIM)
        mine = pl.ds(8, 64)
        total = grad[0, x, mine, :] - grad[0, x + 4, mine, :]
        total += grad[1, x + 2, pl.ds(6, 64), :] - grad[1, x + 2, pl.ds(10, 64), :]
        total += 8.0 * (grad[0, x + 3, mine, :] - grad[0, x + 1, mine, :])
        total += 8.0 * (grad[1, x + 2, pl.ds(9, 64), :] - grad[1, x + 2, pl.ds(7, 64), :])
        third = grad[2, x + 2, mine, :]
        total += jnp.where(lane >= 2, pltpu.roll(third, 2, 1), 0.0)
        total -= jnp.where(lane < 126, pltpu.roll(third, 126, 1), 0.0)
        total += 8.0 * jnp.where(lane < 127, pltpu.roll(third, 127, 1), 0.0)
        total -= 8.0 * jnp.where(lane >= 1, pltpu.roll(third, 1, 1), 0.0)
        curv[x] = total * (1.0 / 12.0) * cells[x // BLOCK]
        return carry

    chunk = 16
    outs = []
    for start in range(0, rows, chunk):
        lax.fori_loop(start, start + chunk, plane, 0, unroll=2)
        number = start // chunk
        for c in range(3):
            outs.append(pltpu.make_async_copy(
                grad.at[c, pl.ds(start + RIM, chunk), pl.ds(8, 64)],
                normals.at[c, pl.ds(start, chunk)], out_sems.at[number, c]))
            outs[-1].start()
        outs.append(pltpu.make_async_copy(
            curv.at[pl.ds(start, chunk)], curvature.at[pl.ds(start, chunk)], out_sems.at[number, 3]))
        outs[-1].start()
    for copy in outs:
        copy.wait()


def shards(level_set, band):
    rows, lines, depth = level_set.shape
    count = lax.axis_size("gx")
    part, core = lax.axis_index("gx"), lax.axis_index("gy")
    forward = [(i, i + 1) for i in range(count - 1)]
    backward = [(i + 1, i) for i in range(count - 1)]
    swap = [(0, 1), (1, 0)]

    def near(block):
        start = jnp.where(core == 0, lines - SIDE, 0)
        return lax.ppermute(lax.dynamic_slice_in_dim(block, start, SIDE, axis=1), "gy", swap)

    low = lax.ppermute(level_set[rows - REACH:], "gx", forward)
    high = lax.ppermute(level_set[:REACH], "gx", backward)
    peer = near(level_set)
    low_peer, high_peer = near(low), near(high)

    here = jnp.arange(depth)
    z_smooth, z_slope = weights(here, here, True)
    z_both = jnp.concatenate([z_smooth, z_slope], axis=0).T
    z_high, z_low = weight_halves(z_both)
    zmat = jnp.concatenate([z_high, z_high, z_low], axis=0)

    slots = jnp.arange(YPAD)
    base = core * lines
    peer_base = jnp.where(core == 0, lines, lines - SIDE)
    source = jnp.where(slots < lines, base + slots, peer_base + slots - lines)
    source = jnp.where(slots < lines + SIDE, source, -10000)
    target = base - 8 + jnp.arange(YOUT)
    inside = ((target >= 0) & (target < 2 * lines))[:, None]
    y_smooth, y_slope = weights(source, target, inside)
    ymat = jnp.concatenate([left_matrix(y_smooth), left_matrix(y_slope)], axis=0)

    start = part * rows
    total = count * rows

    def x_matrix(source, target):
        inside = ((target >= 0) & (target < total))[:, None]
        smooth, slope = weights(source, target, inside)
        return jnp.concatenate([left_matrix(slope), left_matrix(smooth)], axis=0)

    grad_rows = rows + 8
    xmat = x_matrix(start + jnp.arange(rows), start - RIM + jnp.arange(grad_rows))
    place = jnp.arange(2 * SIDE)
    edge_source = jnp.where(place < REACH, start - REACH + place, -10000)
    edge_source = jnp.where((place >= SIDE) & (place < SIDE + REACH), start + rows + place - SIDE, edge_source)
    edge_target = start - RIM + jnp.where(place < SIDE, place, place + rows + 2 * RIM - 2 * SIDE)
    edge_xmat = x_matrix(edge_source, edge_target)

    cells = lax.dynamic_slice(
        band, (part * (rows // BLOCK), core * (lines // BLOCK), 0),
        (rows // BLOCK, lines // BLOCK, band.shape[2])).astype(jnp.float32)
    cells = jnp.repeat(jnp.repeat(cells, BLOCK, axis=1), BLOCK, axis=2)

    vmem, anywhere = pl.BlockSpec(memory_space=pltpu.VMEM), pl.BlockSpec(memory_space=pl.ANY)
    grad = pl.pallas_call(
        functools.partial(local_kernel, rows, grad_rows),
        out_shape=jax.ShapeDtypeStruct((3, grad_rows, YOUT, depth), jnp.float32),
        in_specs=[anywhere, anywhere, vmem, vmem, vmem],
        out_specs=vmem,
        scratch_shapes=[
            pltpu.VMEM((rows * (lines + SIDE), depth), jnp.float32),
            pltpu.VMEM((3, grad_rows * YPAD, depth), jnp.float32),
            pltpu.SemaphoreType.DMA((2,)),
        ],
        compiler_params=pltpu.CompilerParams(vmem_limit_bytes=50 * 2**20),
        cost_estimate=pl.CostEstimate(flops=10**10, bytes_accessed=3 * 10**7, transcendentals=0),
        name="local_part",
    )(level_set, peer, zmat, xmat, ymat)
    return pl.pallas_call(
        functools.partial(edge_kernel, rows),
        out_shape=(
            jax.ShapeDtypeStruct((3, rows, lines, depth), jnp.float32),
            jax.ShapeDtypeStruct((rows, lines, depth), jnp.float32),
        ),
        in_specs=[anywhere] * 5 + [vmem] * 4,
        out_specs=(anywhere, anywhere),
        scratch_shapes=[
            pltpu.VMEM((2 * SIDE * (lines + SIDE), depth), jnp.float32),
            pltpu.VMEM((3, 2 * SIDE * YPAD, depth), jnp.float32),
            pltpu.VMEM((3, grad_rows, YOUT, depth), jnp.float32),
            pltpu.VMEM((rows, lines, depth), jnp.float32),
            pltpu.SemaphoreType.DMA((5,)),
            pltpu.SemaphoreType.DMA((rows // 16, 4)),
        ],
        compiler_params=pltpu.CompilerParams(vmem_limit_bytes=50 * 2**20),
        name="edge_part",
    )(low, high, low_peer, high_peer, grad, cells, zmat, edge_xmat, ymat)


def solution(mesh):
    placed = (P(("groups", "gx"), "gy", None), P("groups", None, None))
    return jax.shard_map(
        shards,
        mesh=mesh,
        in_specs=placed,
        out_specs=(P(None, ("groups", "gx"), "gy", None), P(("groups", "gx"), "gy", None)),
        check_vma=False,
    )
```

```python
import functools

import jax
import jax.numpy as jnp
import ml_dtypes
import numpy as np
from jax import lax
from jax.experimental import pallas as pl
from jax.experimental.pallas import tpu as pltpu
from jax.sharding import PartitionSpec as P

HALF_TAPS = 20
BLOCK = 32
SIGMA_CELLS = 7.0
FLOOR_SQ = 0.05
RIM = 2
REACH = HALF_TAPS + RIM
SIDE = 24
YPAD = 96
YOUT = 80
CHUNKS = ((0, 24), (24, 16), (40, 16), (56, 8))
MESH = pl.DeviceIdType.MESH


def weights(source, target, valid):
    offsets = np.arange(-HALF_TAPS, HALF_TAPS + 1).astype(np.float64)
    bell = np.exp(-offsets * offsets / (2.0 * SIGMA_CELLS * SIGMA_CELLS))
    total = np.sum(bell)
    moment = np.sum(offsets * offsets * (bell / total))
    distance = (source[None, :] - target[:, None]).astype(np.float64)
    inside = (np.abs(distance) <= HALF_TAPS) & valid
    values = np.exp(-np.where(inside, distance, 0.0) ** 2 / (2.0 * SIGMA_CELLS * SIGMA_CELLS)) / total
    values = np.where(inside, values, 0.0)
    return values, distance * values / moment


def weight_halves(values):
    high = values.astype(ml_dtypes.bfloat16)
    return high, (values - high.astype(np.float64)).astype(ml_dtypes.bfloat16)


def wide(values):
    high, low = weight_halves(values)
    return np.concatenate([high, high, low], axis=1)


def tall(values):
    high, low = weight_halves(values)
    return np.concatenate([np.concatenate([high, high], 1), np.concatenate([low, low], 1)], 0)


def halves(values):
    high = values.astype(jnp.bfloat16)
    low = (values - high.astype(jnp.float32)).astype(jnp.bfloat16)
    return high, low


def stack_halves(values):
    return jnp.concatenate(halves(values), axis=0)


def dot(a, b):
    return jnp.dot(a, b, preferred_element_type=jnp.float32)


def clear_pad(mid, planes, width):
    def clear(x, carry):
        for c in range(3):
            mid[c, pl.ds(pl.multiple_of(x * YPAD, 8) + width, YPAD - width), :] = jnp.zeros(
                (YPAD - width, 128), jnp.float32)
        return carry

    lax.fori_loop(0, planes, clear, 0)


def columns(src, rows, out_rows, zmat, xmat, mid, width, first, groups):
    def step(number, carry):
        base = first + number * 8
        lines = [src[pl.ds(base + i, rows, stride=width), :] for i in range(8)]
        high, low = halves(jnp.concatenate(lines, axis=0))
        along_z = dot(jnp.concatenate([high, low, high], axis=1), zmat[...])
        high, low = halves(along_z)
        for i in range(8):
            part = slice(i * rows, (i + 1) * rows)
            both = dot(xmat[...], jnp.concatenate([high[part], low[part], high[part]], axis=0))
            place = pl.ds(base + i, out_rows, stride=YPAD)
            mid[0, place, :] = both[:out_rows, :128]
            mid[1, place, :] = both[out_rows:, :128]
            mid[2, place, :] = both[out_rows:, 128:]
        return carry

    lax.fori_loop(0, groups, step, 0)


def plane(mid, ymat, core, x):
    place = pl.ds(pl.multiple_of(x * YPAD, 8), YPAD)
    first = stack_halves(mid[0, place, :])
    second = stack_halves(mid[1, place, :])
    third = stack_halves(mid[2, place, :])
    smooth = dot(ymat[2 * core], jnp.concatenate([first, third], axis=1))
    smooth = smooth[:YOUT] + smooth[YOUT:]
    slope = dot(ymat[2 * core + 1], second)
    return smooth[:, :128], slope[:YOUT] + slope[YOUT:], smooth[:, 128:]


def gradient_kernel(
    rows, lines, out_rows, count, level, zmat, xmat, edge_xmat, ymat, grad_out,
    own, peer, halo, halo_peer, src, edge_src, mid, edge_mid, grad,
    own_sem, peer_sems, send_sems, recv_sems, corner_send, corner_recv, out_sems
):
    width = lines + SIDE
    group, me, core = lax.axis_index("groups"), lax.axis_index("gx"), lax.axis_index("gy")
    lower, upper = me > 0, me < count - 1
    load = pltpu.make_async_copy(level, own, own_sem)
    load.start()

    barrier = pltpu.get_barrier_semaphore()
    pl.semaphore_signal(barrier, inc=1, device_id=(group, me, 1 - core), device_id_type=MESH)

    @pl.when(lower)
    def _():
        pl.semaphore_signal(barrier, inc=1, device_id=(group, me - 1, core), device_id_type=MESH)

    @pl.when(upper)
    def _():
        pl.semaphore_signal(barrier, inc=1, device_id=(group, me + 1, core), device_id_type=MESH)

    pl.semaphore_wait(barrier, 1 + lower.astype(jnp.int32) + upper.astype(jnp.int32))

    def piece(number):
        offset, size = CHUNKS[number]
        start = jnp.where(core == 0, lines - offset - size, offset)
        return pl.multiple_of(start, 8), size

    near = pl.ds(piece(0)[0], SIDE)
    to_peer = pltpu.make_async_remote_copy(
        level.at[:, near], peer, peer_sems.at[0], peer_sems.at[1],
        device_id=(group, me, 1 - core), device_id_type=MESH)
    to_peer.start()

    def halo_copy(side, number):
        start, size = piece(number)
        cut = pl.ds(rows - REACH, REACH) if side == 0 else pl.ds(0, REACH)
        return pltpu.make_async_remote_copy(
            level.at[cut, pl.ds(start, size)], halo.at[side, :, pl.ds(start, size)],
            send_sems.at[side, number], recv_sems.at[side, number],
            device_id=(group, me + 1 if side == 0 else me - 1, core), device_id_type=MESH)

    for number in range(len(CHUNKS)):
        @pl.when(upper)
        def _():
            halo_copy(0, number).start()

        @pl.when(lower)
        def _():
            halo_copy(1, number).start()

    @pl.when(me == 0)
    def _():
        halo[0] = jnp.zeros((REACH, lines, 128), jnp.float32)
        halo_peer[0] = jnp.zeros((REACH, SIDE, 128), jnp.float32)

    @pl.when(me == count - 1)
    def _():
        halo[1] = jnp.zeros((REACH, lines, 128), jnp.float32)
        halo_peer[1] = jnp.zeros((REACH, SIDE, 128), jnp.float32)

    for side in range(2):
        edge_src[pl.ds((side * SIDE + REACH) * width, (SIDE - REACH) * width), :] = jnp.zeros(
            ((SIDE - REACH) * width, 128), jnp.float32)
    clear_pad(mid, out_rows, width)
    clear_pad(edge_mid, 2 * SIDE, width)

    load.wait()
    to_peer.wait()

    def place_own(x, carry):
        base = pl.multiple_of(x * width, 8)
        src[pl.ds(base, lines), :] = own[x]
        src[pl.ds(base + lines, SIDE), :] = peer[x]
        return carry

    lax.fori_loop(0, rows, place_own, 0)
    columns(src, rows, out_rows, zmat, xmat, mid, width, 0, width // 8)

    def own_plane(x, carry):
        for c, value in enumerate(plane(mid, ymat, core, x)):
            grad[c, x] = value
        return carry

    lax.fori_loop(0, rows + 2 * RIM, own_plane, 0, unroll=4)
    shift = rows + 2 * RIM - 2 * SIDE
    inner = pltpu.make_async_copy(
        grad.at[:, pl.ds(SIDE, shift)], grad_out.at[:, pl.ds(SIDE, shift)], out_sems.at[0])
    inner.start()

    def corner(side):
        return pltpu.make_async_remote_copy(
            halo.at[side, :, near], halo_peer.at[side], corner_send.at[side], corner_recv.at[side],
            device_id=(group, me, 1 - core), device_id_type=MESH)

    def place_edge(ref, start, size, slot):
        def step(x, carry):
            for side in range(2):
                base = pl.multiple_of((side * SIDE + x) * width + slot, 8)
                edge_src[pl.ds(base, size), :] = ref[side, x, pl.ds(start, size), :]
            return carry

        lax.fori_loop(0, REACH, step, 0)

    def edge_columns(slot, size):
        columns(edge_src, 2 * SIDE, 2 * SIDE, zmat, edge_xmat, edge_mid, width, slot, size // 8)

    for number in range(len(CHUNKS)):
        start, size = piece(number)

        @pl.when(lower)
        def _():
            halo_copy(0, number).wait_recv()
            if number == 0:
                corner(0).start()

        @pl.when(upper)
        def _():
            halo_copy(1, number).wait_recv()
            if number == 0:
                corner(1).start()

        place_edge(halo, start, size, start)
        edge_columns(start, size)
        if number == 1:
            @pl.when(lower)
            def _():
                corner(0).wait()

            @pl.when(upper)
            def _():
                corner(1).wait()

            place_edge(halo_peer, 0, SIDE, lines)
            edge_columns(lines, SIDE)

    outs = [inner]
    for number in range(2 * SIDE // 8):
        offset = 0 if number * 8 < SIDE else shift

        def edge_plane(x, carry):
            for c, value in enumerate(plane(edge_mid, ymat, core, x)):
                grad[c, x + offset] += value
            return carry

        lax.fori_loop(number * 8, number * 8 + 8, edge_plane, 0, unroll=4)
        done = pl.ds(number * 8 + offset, 8)
        outs.append(pltpu.make_async_copy(grad.at[:, done], grad_out.at[:, done], out_sems.at[number + 1]))
        outs[-1].start()
    for copy in outs:
        copy.wait()
    for number in range(len(CHUNKS)):
        @pl.when(upper)
        def _():
            halo_copy(0, number).wait_send()

        @pl.when(lower)
        def _():
            halo_copy(1, number).wait_send()


def normals_kernel(rows, lines, count, band, grad_in, normals, curvature, grad, curv, in_sems, out_sems):
    me, core = lax.axis_index("gx"), lax.axis_index("gy")
    chunk = 16
    loads = []
    for number in range(rows // chunk):
        span = pl.ds(0, chunk + 2 * RIM) if number == 0 else pl.ds(number * chunk + 2 * RIM, chunk)
        loads.append(pltpu.make_async_copy(grad_in.at[:, span], grad.at[:, span], in_sems.at[number]))
        loads[-1].start()

    lane = lax.broadcasted_iota(jnp.int32, (BLOCK, 128), 1)

    def cells(block_x):
        parts = []
        for block_y in range(lines // BLOCK):
            base = ((me * (rows // BLOCK) + block_x) * 2 + core) * (lines // BLOCK) + block_y
            listed = jnp.zeros((BLOCK, 128), jnp.float32)
            for block_z in range(128 // BLOCK):
                value = band[base * (128 // BLOCK) + block_z].astype(jnp.float32) * (1.0 / 12.0)
                listed = jnp.where(lane // BLOCK == block_z, value, listed)
            parts.append(listed)
        return jnp.concatenate(parts, axis=0)

    def unit(x):
        first, second, third = grad[0, x], grad[1, x], grad[2, x]
        inverse = lax.rsqrt(jnp.maximum(first * first + second * second + third * third, FLOOR_SQ))
        grad[0, x] = first * inverse
        grad[1, x] = second * inverse
        grad[2, x] = third * inverse

    position = lax.broadcasted_iota(jnp.int32, (lines, 128), 1)
    mine = pl.ds(8, lines)

    def outside(first):
        for x in range(first, first + RIM):
            grad[0, x] = jnp.zeros((YOUT, 128), jnp.float32)

    outs = []
    for number in range(rows // chunk):
        start = number * chunk
        loads[number].wait()
        if number == 0:
            for x in range(2 * RIM):
                unit(x)
            pl.when(me == 0)(functools.partial(outside, 0))
        listed = cells(start // BLOCK)

        def units(x, carry):
            unit(x)
            return carry

        lax.fori_loop(start + 2 * RIM, start + 2 * RIM + chunk, units, 0, unroll=4)
        if number == rows // chunk - 1:
            pl.when(me == count - 1)(functools.partial(outside, rows + RIM))

        def divergence(x, carry):
            total = grad[0, x, mine, :] - grad[0, x + 4, mine, :]
            total += grad[1, x + 2, pl.ds(6, lines), :] - grad[1, x + 2, pl.ds(10, lines), :]
            third = grad[2, x + 2, mine, :]
            total += jnp.where(position >= 2, pltpu.roll(third, 2, 1), 0.0)
            total -= jnp.where(position < 126, pltpu.roll(third, 126, 1), 0.0)
            near = grad[0, x + 3, mine, :] - grad[0, x + 1, mine, :]
            near += grad[1, x + 2, pl.ds(9, lines), :] - grad[1, x + 2, pl.ds(7, lines), :]
            near += jnp.where(position < 127, pltpu.roll(third, 127, 1), 0.0)
            near -= jnp.where(position >= 1, pltpu.roll(third, 1, 1), 0.0)
            curv[x] = (total + 8.0 * near) * listed
            return carry

        lax.fori_loop(start, start + chunk, divergence, 0, unroll=2)
        for c in range(3):
            outs.append(pltpu.make_async_copy(
                grad.at[c, pl.ds(start + RIM, chunk), mine],
                normals.at[c, pl.ds(start, chunk)], out_sems.at[number, c]))
            outs[-1].start()
        outs.append(pltpu.make_async_copy(
            curv.at[pl.ds(start, chunk)], curvature.at[pl.ds(start, chunk)], out_sems.at[number, 3]))
        outs[-1].start()
    for copy in outs:
        copy.wait()


def shards(level_set, band):
    rows, lines, depth = level_set.shape
    count = lax.axis_size("gx")
    width = lines + SIDE

    here = np.arange(depth)
    z_high, z_low = weight_halves(np.concatenate(weights(here, here, True), axis=0).T)
    zmat = np.concatenate([z_high, z_high, z_low], axis=0)

    def x_matrix(source, target):
        smooth, slope = weights(source, target, True)
        return np.concatenate([wide(slope), wide(smooth)], axis=0)

    out_rows = rows + 8
    far = -10000
    place = np.arange(2 * SIDE)
    edge_source = np.where(place < REACH, place - REACH, far)
    edge_source = np.where((place >= SIDE) & (place < SIDE + REACH), rows + place - SIDE, edge_source)
    edge_target = np.where(place < SIDE, place, place + rows + 2 * RIM - 2 * SIDE) - RIM
    xmat = x_matrix(np.arange(rows), np.arange(out_rows) - RIM)
    edge_xmat = x_matrix(edge_source, edge_target)

    slots = np.arange(YPAD)
    ymats = []
    for core in range(2):
        base = core * lines
        peer_base = lines if core == 0 else lines - SIDE
        source = np.where(slots < lines, base + slots, peer_base + slots - lines)
        source = np.where(slots < width, source, far)
        target = base - 8 + np.arange(YOUT)
        inside = ((target >= 0) & (target < 2 * lines))[:, None]
        ymats += [tall(values) for values in weights(source, target, inside)]
    ymat = np.stack(ymats)

    vmem, anywhere = pl.BlockSpec(memory_space=pltpu.VMEM), pl.BlockSpec(memory_space=pl.ANY)
    grad = pl.pallas_call(
        functools.partial(gradient_kernel, rows, lines, out_rows, count),
        out_shape=jax.ShapeDtypeStruct((3, out_rows, YOUT, depth), jnp.float32),
        in_specs=[anywhere] + [vmem] * 4,
        out_specs=anywhere,
        scratch_shapes=[
            pltpu.VMEM((rows, lines, depth), jnp.float32),
            pltpu.VMEM((rows, SIDE, depth), jnp.float32),
            pltpu.VMEM((2, REACH, lines, depth), jnp.float32),
            pltpu.VMEM((2, REACH, SIDE, depth), jnp.float32),
            pltpu.VMEM((rows * width, depth), jnp.float32),
            pltpu.VMEM((2 * SIDE * width, depth), jnp.float32),
            pltpu.VMEM((3, out_rows * YPAD, depth), jnp.float32),
            pltpu.VMEM((3, 2 * SIDE * YPAD, depth), jnp.float32),
            pltpu.VMEM((3, out_rows, YOUT, depth), jnp.float32),
            pltpu.SemaphoreType.DMA,
            pltpu.SemaphoreType.DMA((2,)),
            pltpu.SemaphoreType.DMA((2, len(CHUNKS))),
            pltpu.SemaphoreType.DMA((2, len(CHUNKS))),
            pltpu.SemaphoreType.DMA((2,)),
            pltpu.SemaphoreType.DMA((2,)),
            pltpu.SemaphoreType.DMA((2 * SIDE // 8 + 1,)),
        ],
        compiler_params=pltpu.CompilerParams(
            vmem_limit_bytes=50 * 2**20, collective_id=0, has_side_effects=True),
        name="gradients",
    )(level_set, *(jnp.asarray(matrix) for matrix in (zmat, xmat, edge_xmat, ymat)))
    return pl.pallas_call(
        functools.partial(normals_kernel, rows, lines, count),
        out_shape=(
            jax.ShapeDtypeStruct((3, rows, lines, depth), jnp.float32),
            jax.ShapeDtypeStruct((rows, lines, depth), jnp.float32),
        ),
        in_specs=[pl.BlockSpec(memory_space=pltpu.SMEM), anywhere],
        out_specs=(anywhere, anywhere),
        scratch_shapes=[
            pltpu.VMEM((3, out_rows, YOUT, depth), jnp.float32),
            pltpu.VMEM((rows, lines, depth), jnp.float32),
            pltpu.SemaphoreType.DMA((rows // 16,)),
            pltpu.SemaphoreType.DMA((rows // 16, 4)),
        ],
        compiler_params=pltpu.CompilerParams(vmem_limit_bytes=40 * 2**20),
        name="normals_and_divergence",
    )(band.reshape(-1), grad)


def solution(mesh):
    placed = (P(("groups", "gx"), "gy", None), P("groups", None, None))
    return jax.shard_map(
        shards,
        mesh=mesh,
        in_specs=placed,
        out_specs=(P(None, ("groups", "gx"), "gy", None), P(("groups", "gx"), "gy", None)),
        check_vma=False,
    )
```

```python
import functools

import jax
import jax.numpy as jnp
import ml_dtypes
import numpy as np
from jax import lax
from jax.experimental import pallas as pl
from jax.experimental.pallas import tpu as pltpu
from jax.sharding import PartitionSpec as P

HALF_TAPS = 20
BLOCK = 32
SIGMA_CELLS = 7.0
FLOOR_SQ = 0.05
RIM = 2
REACH = HALF_TAPS + RIM
SIDE = 24
YPAD = 96
YOUT = 80
VMEM_BYTES = 63 * 2**20
CHUNKS = ((0, 24), (24, 16), (40, 16), (56, 8))
MESH = pl.DeviceIdType.MESH


def weights(source, target, valid):
    offsets = np.arange(-HALF_TAPS, HALF_TAPS + 1).astype(np.float64)
    bell = np.exp(-offsets * offsets / (2.0 * SIGMA_CELLS * SIGMA_CELLS))
    total = np.sum(bell)
    moment = np.sum(offsets * offsets * (bell / total))
    distance = (source[None, :] - target[:, None]).astype(np.float64)
    inside = (np.abs(distance) <= HALF_TAPS) & valid
    values = np.exp(-np.where(inside, distance, 0.0) ** 2 / (2.0 * SIGMA_CELLS * SIGMA_CELLS)) / total
    values = np.where(inside, values, 0.0)
    return values, distance * values / moment


def weight_halves(values):
    high = values.astype(ml_dtypes.bfloat16)
    return high, (values - high.astype(np.float64)).astype(ml_dtypes.bfloat16)


def wide(values):
    high, low = weight_halves(values)
    return np.concatenate([high, high, low], axis=1)


def tall(values):
    high, low = weight_halves(values)
    return np.concatenate([np.concatenate([high, high], 1), np.concatenate([low, low], 1)], 0)


def halves(values):
    high = values.astype(jnp.bfloat16)
    low = (values - high.astype(jnp.float32)).astype(jnp.bfloat16)
    return high, low


def stack_halves(values):
    return jnp.concatenate(halves(values), axis=0)


def dot(a, b):
    return jnp.dot(a, b, preferred_element_type=jnp.float32)


def clear_pad(mid, planes, width):
    def clear(x, carry):
        for c in range(3):
            mid[c, pl.ds(pl.multiple_of(x * YPAD, 8) + width, YPAD - width), :] = jnp.zeros(
                (YPAD - width, 128), jnp.float32)
        return carry

    lax.fori_loop(0, planes, clear, 0)


def columns(src, rows, out_rows, zmat, xmat, mid, width, first, groups):
    def step(number, carry):
        base = first + number * 8
        lines = [src[pl.ds(base + i, rows, stride=width), :] for i in range(8)]
        high, low = halves(jnp.concatenate(lines, axis=0))
        along_z = dot(jnp.concatenate([high, low, high], axis=1), zmat[...])
        high, low = halves(along_z)
        for i in range(8):
            part = slice(i * rows, (i + 1) * rows)
            both = dot(xmat[...], jnp.concatenate([high[part], low[part], high[part]], axis=0))
            place = pl.ds(base + i, out_rows, stride=YPAD)
            mid[0, place, :] = both[:out_rows, :128]
            mid[1, place, :] = both[out_rows:, :128]
            mid[2, place, :] = both[out_rows:, 128:]
        return carry

    lax.fori_loop(0, groups, step, 0)


def plane(mid, ymat, core, x):
    place = pl.ds(pl.multiple_of(x * YPAD, 8), YPAD)
    first = stack_halves(mid[0, place, :])
    second = stack_halves(mid[1, place, :])
    third = stack_halves(mid[2, place, :])
    smooth = dot(ymat[2 * core], jnp.concatenate([first, third], axis=1))
    smooth = smooth[:YOUT] + smooth[YOUT:]
    slope = dot(ymat[2 * core + 1], second)
    return smooth[:, :128], slope[:YOUT] + slope[YOUT:], smooth[:, 128:]


def unit(grad, x):
    first, second, third = grad[0, x], grad[1, x], grad[2, x]
    inverse = lax.rsqrt(jnp.maximum(first * first + second * second + third * third, FLOOR_SQ))
    grad[0, x] = first * inverse
    grad[1, x] = second * inverse
    grad[2, x] = third * inverse


def divergence(normal, x, lines):
    mine = pl.ds(8, lines)
    position = lax.broadcasted_iota(jnp.int32, (lines, 128), 1)
    total = normal[0, x, mine, :] - normal[0, x + 4, mine, :]
    total += normal[1, x + 2, pl.ds(6, lines), :] - normal[1, x + 2, pl.ds(10, lines), :]
    third = normal[2, x + 2, mine, :]
    total += jnp.where(position >= 2, pltpu.roll(third, 2, 1), 0.0)
    total -= jnp.where(position < 126, pltpu.roll(third, 126, 1), 0.0)
    near = normal[0, x + 3, mine, :] - normal[0, x + 1, mine, :]
    near += normal[1, x + 2, pl.ds(9, lines), :] - normal[1, x + 2, pl.ds(7, lines), :]
    near += jnp.where(position < 127, pltpu.roll(third, 127, 1), 0.0)
    near -= jnp.where(position >= 1, pltpu.roll(third, 1, 1), 0.0)
    return total + 8.0 * near


def listed_cells(band, me, core, block_x, rows, lines):
    lane = lax.broadcasted_iota(jnp.int32, (BLOCK, 128), 1)
    parts = []
    for block_y in range(lines // BLOCK):
        listed = jnp.zeros((BLOCK, 128), jnp.float32)
        for block_z in range(128 // BLOCK):
            value = band[core * (lines // BLOCK) + block_y, block_z, me * (rows // BLOCK) + block_x]
            listed = jnp.where(lane // BLOCK == block_z, value.astype(jnp.float32) * (1.0 / 12.0), listed)
        parts.append(listed)
    return jnp.concatenate(parts, axis=0)


def gradient_kernel(
    rows, lines, out_rows, count, level, band, zmat_in, xmat_in, edge_xmat_in, ymat_in, grad_out, inner_out,
    own, peer, halo, halo_peer, src, edge_src, mid, edge_mid, grad, inner_curv,
    zmat, xmat, edge_xmat, ymat, zmat_wide, xmat_wide, edge_xmat_wide, ymat_wide,
    own_sem, matrix_sems, peer_sems, send_sems, recv_sems, corner_send, corner_recv, out_sems
):
    width = lines + SIDE
    group, me, core = lax.axis_index("groups"), lax.axis_index("gx"), lax.axis_index("gy")
    lower, upper = me > 0, me < count - 1
    load = pltpu.make_async_copy(level, own, own_sem)
    load.start()
    matrices = (
        (zmat_in, zmat_wide, zmat), (xmat_in, xmat_wide, xmat),
        (edge_xmat_in, edge_xmat_wide, edge_xmat), (ymat_in, ymat_wide, ymat))
    matrix_loads = [
        pltpu.make_async_copy(source, target, matrix_sems.at[number])
        for number, (source, target, _) in enumerate(matrices)]
    for copy in matrix_loads:
        copy.start()

    barrier = pltpu.get_barrier_semaphore()
    pl.semaphore_signal(barrier, inc=1, device_id=(group, me, 1 - core), device_id_type=MESH)

    @pl.when(lower)
    def _():
        pl.semaphore_signal(barrier, inc=1, device_id=(group, me - 1, core), device_id_type=MESH)

    @pl.when(upper)
    def _():
        pl.semaphore_signal(barrier, inc=1, device_id=(group, me + 1, core), device_id_type=MESH)

    pl.semaphore_wait(barrier, 1 + lower.astype(jnp.int32) + upper.astype(jnp.int32))

    def piece(number):
        offset, size = CHUNKS[number]
        start = jnp.where(core == 0, lines - offset - size, offset)
        return pl.multiple_of(start, 8), size

    near = pl.ds(piece(0)[0], SIDE)
    to_peer = pltpu.make_async_remote_copy(
        level.at[:, near], peer, peer_sems.at[0], peer_sems.at[1],
        device_id=(group, me, 1 - core), device_id_type=MESH)
    to_peer.start()

    def halo_copy(side, number):
        start, size = piece(number)
        cut = pl.ds(rows - REACH, REACH) if side == 0 else pl.ds(0, REACH)
        return pltpu.make_async_remote_copy(
            level.at[cut, pl.ds(start, size)], halo.at[side, :, pl.ds(start, size)],
            send_sems.at[side, number], recv_sems.at[side, number],
            device_id=(group, me + 1 if side == 0 else me - 1, core), device_id_type=MESH)

    for number in range(len(CHUNKS)):
        @pl.when(upper)
        def _():
            halo_copy(0, number).start()

        @pl.when(lower)
        def _():
            halo_copy(1, number).start()

    @pl.when(me == 0)
    def _():
        halo[0] = jnp.zeros((REACH, lines, 128), jnp.float32)
        halo_peer[0] = jnp.zeros((REACH, SIDE, 128), jnp.float32)

    @pl.when(me == count - 1)
    def _():
        halo[1] = jnp.zeros((REACH, lines, 128), jnp.float32)
        halo_peer[1] = jnp.zeros((REACH, SIDE, 128), jnp.float32)

    for side in range(2):
        edge_src[pl.ds((side * SIDE + REACH) * width, (SIDE - REACH) * width), :] = jnp.zeros(
            ((SIDE - REACH) * width, 128), jnp.float32)
    clear_pad(mid, out_rows, width)
    clear_pad(edge_mid, 2 * SIDE, width)

    for copy, (_, source, target) in zip(matrix_loads, matrices):
        copy.wait()
        target[...] = source[...].astype(jnp.bfloat16)
    load.wait()
    to_peer.wait()

    def place_own(x, carry):
        base = pl.multiple_of(x * width, 8)
        src[pl.ds(base, lines), :] = own[x]
        src[pl.ds(base + lines, SIDE), :] = peer[x]
        return carry

    lax.fori_loop(0, rows, place_own, 0)
    columns(src, rows, out_rows, zmat, xmat, mid, width, 0, width // 8)

    def own_plane(x, carry):
        for c, value in enumerate(plane(mid, ymat, core, x)):
            grad[c, x] = value
        return carry

    lax.fori_loop(0, rows + 2 * RIM, own_plane, 0, unroll=4)
    shift = rows + 2 * RIM - 2 * SIDE

    def inner_unit(x, carry):
        unit(grad, x)
        return carry

    lax.fori_loop(SIDE, SIDE + shift, inner_unit, 0, unroll=4)
    inner_rows = shift - 2 * RIM
    for first in range(SIDE, SIDE + inner_rows, 8):
        listed = listed_cells(band, me, core, first // BLOCK, rows, lines)

        def inner_divergence(x, carry):
            inner_curv[x - SIDE] = divergence(grad, x, lines) * listed
            return carry

        lax.fori_loop(first, first + 8, inner_divergence, 0, unroll=2)
    inner = pltpu.make_async_copy(
        grad.at[:, pl.ds(SIDE, shift)], grad_out.at[:, pl.ds(SIDE, shift)], out_sems.at[0])
    inner.start()
    inner_done = pltpu.make_async_copy(inner_curv, inner_out, out_sems.at[2 * SIDE // 8 + 1])
    inner_done.start()

    def corner(side):
        return pltpu.make_async_remote_copy(
            halo.at[side, :, near], halo_peer.at[side], corner_send.at[side], corner_recv.at[side],
            device_id=(group, me, 1 - core), device_id_type=MESH)

    def place_edge(ref, start, size, slot):
        def step(x, carry):
            for side in range(2):
                base = pl.multiple_of((side * SIDE + x) * width + slot, 8)
                edge_src[pl.ds(base, size), :] = ref[side, x, pl.ds(start, size), :]
            return carry

        lax.fori_loop(0, REACH, step, 0)

    def edge_columns(slot, size):
        columns(edge_src, 2 * SIDE, 2 * SIDE, zmat, edge_xmat, edge_mid, width, slot, size // 8)

    for number in range(len(CHUNKS)):
        start, size = piece(number)

        @pl.when(lower)
        def _():
            halo_copy(0, number).wait_recv()
            if number == 0:
                corner(0).start()

        @pl.when(upper)
        def _():
            halo_copy(1, number).wait_recv()
            if number == 0:
                corner(1).start()

        place_edge(halo, start, size, start)
        edge_columns(start, size)
        if number == 1:
            @pl.when(lower)
            def _():
                corner(0).wait()

            @pl.when(upper)
            def _():
                corner(1).wait()

            place_edge(halo_peer, 0, SIDE, lines)
            edge_columns(lines, SIDE)

    outs = [inner, inner_done]
    for number in range(2 * SIDE // 8):
        offset = 0 if number * 8 < SIDE else shift

        def edge_plane(x, carry):
            for c, value in enumerate(plane(edge_mid, ymat, core, x)):
                grad[c, x + offset] += value
            return carry

        lax.fori_loop(number * 8, number * 8 + 8, edge_plane, 0, unroll=4)
        done = pl.ds(number * 8 + offset, 8)
        outs.append(pltpu.make_async_copy(grad.at[:, done], grad_out.at[:, done], out_sems.at[number + 1]))
        outs[-1].start()
    for copy in outs:
        copy.wait()
    for number in range(len(CHUNKS)):
        @pl.when(upper)
        def _():
            halo_copy(0, number).wait_send()

        @pl.when(lower)
        def _():
            halo_copy(1, number).wait_send()


def normals_kernel(
    rows, lines, count, band, grad_in, inner_in, normals, curvature, grad, curv, in_sems, out_sems, inner_sems
):
    me, core = lax.axis_index("gx"), lax.axis_index("gy")
    mine = pl.ds(8, lines)
    inner_rows = rows - 2 * SIDE
    cut = SIDE + 2 * RIM
    spans = [(0, 12), (12, 8), (20, 8), (cut + inner_rows - 2 * RIM, 12), (cut + inner_rows + 8, 8),
             (cut + inner_rows + 16, 8)]
    loads = []
    for number, (first, size) in enumerate(spans):
        span = pl.ds(first, size)
        loads.append(pltpu.make_async_copy(grad_in.at[:, span], grad.at[:, span], in_sems.at[number]))
        loads[-1].start()
    outs = []
    for c in range(3):
        outs.append(pltpu.make_async_copy(
            grad_in.at[c, pl.ds(SIDE + RIM, inner_rows), mine],
            normals.at[c, pl.ds(SIDE, inner_rows)], inner_sems.at[c]))
    outs.append(pltpu.make_async_copy(inner_in, curvature.at[pl.ds(SIDE, inner_rows)], inner_sems.at[3]))
    for copy in outs:
        copy.start()

    def outside(first):
        for x in range(first, first + RIM):
            grad[0, x] = jnp.zeros((YOUT, 128), jnp.float32)

    starts = [0, 8, 16, rows - 24, rows - 16, rows - 8]
    for number, start in enumerate(starts):
        loads[number].wait()
        first, size = spans[number]
        low = max(first, SIDE + inner_rows + 2 * RIM) if number >= 3 else first
        high = min(first + size, SIDE) if number < 3 else first + size

        def units(x, carry):
            unit(grad, x)
            return carry

        lax.fori_loop(low, high, units, 0, unroll=4)
        if number == 0:
            pl.when(me == 0)(functools.partial(outside, 0))
        if number == len(starts) - 1:
            pl.when(me == count - 1)(functools.partial(outside, rows + RIM))
        listed = listed_cells(band, me, core, start // BLOCK, rows, lines)

        def finish(x, carry):
            curv[x] = divergence(grad, x, lines) * listed
            return carry

        lax.fori_loop(start, start + 8, finish, 0, unroll=2)
        for c in range(3):
            outs.append(pltpu.make_async_copy(
                grad.at[c, pl.ds(start + RIM, 8), mine],
                normals.at[c, pl.ds(start, 8)], out_sems.at[number, c]))
            outs[-1].start()
        outs.append(pltpu.make_async_copy(
            curv.at[pl.ds(start, 8)], curvature.at[pl.ds(start, 8)], out_sems.at[number, 3]))
        outs[-1].start()
    for copy in outs:
        copy.wait()


def shards(level_set, band):
    rows, lines, depth = level_set.shape
    count = lax.axis_size("gx")
    width = lines + SIDE

    here = np.arange(depth)
    z_high, z_low = weight_halves(np.concatenate(weights(here, here, True), axis=0).T)
    zmat = np.concatenate([z_high, z_high, z_low], axis=0)

    def x_matrix(source, target):
        smooth, slope = weights(source, target, True)
        return np.concatenate([wide(slope), wide(smooth)], axis=0)

    out_rows = rows + 8
    far = -10000
    place = np.arange(2 * SIDE)
    edge_source = np.where(place < REACH, place - REACH, far)
    edge_source = np.where((place >= SIDE) & (place < SIDE + REACH), rows + place - SIDE, edge_source)
    edge_target = np.where(place < SIDE, place, place + rows + 2 * RIM - 2 * SIDE) - RIM
    xmat = x_matrix(np.arange(rows), np.arange(out_rows) - RIM)
    edge_xmat = x_matrix(edge_source, edge_target)

    slots = np.arange(YPAD)
    ymats = []
    for core in range(2):
        base = core * lines
        peer_base = lines if core == 0 else lines - SIDE
        source = np.where(slots < lines, base + slots, peer_base + slots - lines)
        source = np.where(slots < width, source, far)
        target = base - 8 + np.arange(YOUT)
        inside = ((target >= 0) & (target < 2 * lines))[:, None]
        ymats += [tall(values) for values in weights(source, target, inside)]
    ymat = np.stack(ymats)

    anywhere = pl.BlockSpec(memory_space=pl.ANY)
    smem = pl.BlockSpec(memory_space=pltpu.SMEM)
    blocks = jnp.transpose(band, (1, 2, 0))
    matrices = [matrix.astype(np.float32) for matrix in (zmat, xmat, edge_xmat, ymat)]
    inner_rows = rows - 2 * SIDE
    grad, inner = pl.pallas_call(
        functools.partial(gradient_kernel, rows, lines, out_rows, count),
        out_shape=(
            jax.ShapeDtypeStruct((3, out_rows, YOUT, depth), jnp.float32),
            jax.ShapeDtypeStruct((inner_rows, lines, depth), jnp.float32),
        ),
        in_specs=[anywhere, smem] + [anywhere] * 4,
        out_specs=(anywhere, anywhere),
        scratch_shapes=[
            pltpu.VMEM((rows, lines, depth), jnp.float32),
            pltpu.VMEM((rows, SIDE, depth), jnp.float32),
            pltpu.VMEM((2, REACH, lines, depth), jnp.float32),
            pltpu.VMEM((2, REACH, SIDE, depth), jnp.float32),
            pltpu.VMEM((rows * width, depth), jnp.float32),
            pltpu.VMEM((2 * SIDE * width, depth), jnp.float32),
            pltpu.VMEM((3, out_rows * YPAD, depth), jnp.float32),
            pltpu.VMEM((3, 2 * SIDE * YPAD, depth), jnp.float32),
            pltpu.VMEM((3, out_rows, YOUT, depth), jnp.float32),
            pltpu.VMEM((inner_rows, lines, depth), jnp.float32),
            *(pltpu.VMEM(matrix.shape, jnp.bfloat16) for matrix in matrices),
            *(pltpu.VMEM(matrix.shape, jnp.float32) for matrix in matrices),
            pltpu.SemaphoreType.DMA,
            pltpu.SemaphoreType.DMA((4,)),
            pltpu.SemaphoreType.DMA((2,)),
            pltpu.SemaphoreType.DMA((2, len(CHUNKS))),
            pltpu.SemaphoreType.DMA((2, len(CHUNKS))),
            pltpu.SemaphoreType.DMA((2,)),
            pltpu.SemaphoreType.DMA((2,)),
            pltpu.SemaphoreType.DMA((2 * SIDE // 8 + 2,)),
        ],
        compiler_params=pltpu.CompilerParams(
            vmem_limit_bytes=VMEM_BYTES, collective_id=0, has_side_effects=True),
        name="gradients",
    )(level_set, blocks, *(jnp.asarray(matrix) for matrix in matrices))
    return pl.pallas_call(
        functools.partial(normals_kernel, rows, lines, count),
        out_shape=(
            jax.ShapeDtypeStruct((3, rows, lines, depth), jnp.float32),
            jax.ShapeDtypeStruct((rows, lines, depth), jnp.float32),
        ),
        in_specs=[smem, anywhere, anywhere],
        out_specs=(anywhere, anywhere),
        scratch_shapes=[
            pltpu.VMEM((3, out_rows, YOUT, depth), jnp.float32),
            pltpu.VMEM((rows, lines, depth), jnp.float32),
            pltpu.SemaphoreType.DMA((6,)),
            pltpu.SemaphoreType.DMA((6, 4)),
            pltpu.SemaphoreType.DMA((4,)),
        ],
        compiler_params=pltpu.CompilerParams(vmem_limit_bytes=VMEM_BYTES),
        name="normals_and_divergence",
    )(blocks, grad, inner)


def solution(mesh):
    placed = (P(("groups", "gx"), "gy", None), P("groups", None, None))
    return jax.shard_map(
        shards,
        mesh=mesh,
        in_specs=placed,
        out_specs=(P(None, ("groups", "gx"), "gy", None), P(("groups", "gx"), "gy", None)),
        check_vma=False,
    )
```

```python
import functools

import jax
import jax.numpy as jnp
import ml_dtypes
import numpy as np
from jax import lax
from jax.experimental import pallas as pl
from jax.experimental.pallas import tpu as pltpu
from jax.sharding import PartitionSpec as P

HALF_TAPS = 20
BLOCK = 32
SIGMA_CELLS = 7.0
FLOOR_SQ = 0.05
RIM = 2
REACH = HALF_TAPS + RIM
SIDE = 24
YPAD = 96
YOUT = 80
VMEM_BYTES = 63 * 2**20
CHUNKS = ((0, 24), (24, 16), (40, 16), (56, 8))
MESH = pl.DeviceIdType.MESH


def weights(source, target, valid):
    offsets = np.arange(-HALF_TAPS, HALF_TAPS + 1).astype(np.float64)
    bell = np.exp(-offsets * offsets / (2.0 * SIGMA_CELLS * SIGMA_CELLS))
    total = np.sum(bell)
    moment = np.sum(offsets * offsets * (bell / total))
    distance = (source[None, :] - target[:, None]).astype(np.float64)
    inside = (np.abs(distance) <= HALF_TAPS) & valid
    values = np.exp(-np.where(inside, distance, 0.0) ** 2 / (2.0 * SIGMA_CELLS * SIGMA_CELLS)) / total
    values = np.where(inside, values, 0.0)
    return values, distance * values / moment


def weight_halves(values):
    high = values.astype(ml_dtypes.bfloat16)
    return high, (values - high.astype(np.float64)).astype(ml_dtypes.bfloat16)


def wide(values):
    high, low = weight_halves(values)
    return np.concatenate([high, high, low], axis=1)


def tall(values):
    high, low = weight_halves(values)
    return np.concatenate([np.concatenate([high, high], 1), np.concatenate([low, low], 1)], 0)


def halves(values):
    high = values.astype(jnp.bfloat16)
    low = (values - high.astype(jnp.float32)).astype(jnp.bfloat16)
    return high, low


def stack_halves(values):
    return jnp.concatenate(halves(values), axis=0)


def dot(a, b):
    return jnp.dot(a, b, preferred_element_type=jnp.float32)


def clear_pad(mid, planes, width):
    def clear(x, carry):
        for c in range(3):
            mid[c, pl.ds(pl.multiple_of(x * YPAD, 8) + width, YPAD - width), :] = jnp.zeros(
                (YPAD - width, 128), jnp.float32)
        return carry

    lax.fori_loop(0, planes, clear, 0)


def columns(src, rows, out_rows, zmat, xmat, mid, width, first, groups):
    def step(number, carry):
        base = first + number * 8
        lines = [src[pl.ds(base + i, rows, stride=width), :] for i in range(8)]
        high, low = halves(jnp.concatenate(lines, axis=0))
        along_z = dot(jnp.concatenate([high, low, high], axis=1), zmat[...])
        high, low = halves(along_z)
        for i in range(8):
            part = slice(i * rows, (i + 1) * rows)
            both = dot(xmat[...], jnp.concatenate([high[part], low[part], high[part]], axis=0))
            place = pl.ds(base + i, out_rows, stride=YPAD)
            mid[0, place, :] = both[:out_rows, :128]
            mid[1, place, :] = both[out_rows:, :128]
            mid[2, place, :] = both[out_rows:, 128:]
        return carry

    lax.fori_loop(0, groups, step, 0)


def plane(mid, ymat, core, x):
    place = pl.ds(pl.multiple_of(x * YPAD, 8), YPAD)
    first = stack_halves(mid[0, place, :])
    second = stack_halves(mid[1, place, :])
    third = stack_halves(mid[2, place, :])
    smooth = dot(ymat[2 * core], jnp.concatenate([first, third], axis=1))
    smooth = smooth[:YOUT] + smooth[YOUT:]
    slope = dot(ymat[2 * core + 1], second)
    return smooth[:, :128], slope[:YOUT] + slope[YOUT:], smooth[:, 128:]


def unit(grad, x):
    first, second, third = grad[0, x], grad[1, x], grad[2, x]
    inverse = lax.rsqrt(jnp.maximum(first * first + second * second + third * third, FLOOR_SQ))
    grad[0, x] = first * inverse
    grad[1, x] = second * inverse
    grad[2, x] = third * inverse


def divergence(normal, x, lines):
    mine = pl.ds(8, lines)
    position = lax.broadcasted_iota(jnp.int32, (lines, 128), 1)
    total = normal[0, x, mine, :] - normal[0, x + 4, mine, :]
    total += normal[1, x + 2, pl.ds(6, lines), :] - normal[1, x + 2, pl.ds(10, lines), :]
    third = normal[2, x + 2, mine, :]
    total += jnp.where(position >= 2, pltpu.roll(third, 2, 1), 0.0)
    total -= jnp.where(position < 126, pltpu.roll(third, 126, 1), 0.0)
    near = normal[0, x + 3, mine, :] - normal[0, x + 1, mine, :]
    near += normal[1, x + 2, pl.ds(9, lines), :] - normal[1, x + 2, pl.ds(7, lines), :]
    near += jnp.where(position < 127, pltpu.roll(third, 127, 1), 0.0)
    near -= jnp.where(position >= 1, pltpu.roll(third, 1, 1), 0.0)
    return total + 8.0 * near


def listed_cells(band, me, core, block_x, rows, lines):
    lane = lax.broadcasted_iota(jnp.int32, (BLOCK, 128), 1)
    parts = []
    for block_y in range(lines // BLOCK):
        listed = jnp.zeros((BLOCK, 128), jnp.float32)
        for block_z in range(128 // BLOCK):
            value = band[core * (lines // BLOCK) + block_y, block_z, me * (rows // BLOCK) + block_x]
            listed = jnp.where(lane // BLOCK == block_z, value.astype(jnp.float32) * (1.0 / 12.0), listed)
        parts.append(listed)
    return jnp.concatenate(parts, axis=0)


def gradient_kernel(
    rows, lines, out_rows, count, level, band, zmat_in, xmat_in, edge_xmat_in, ymat_in, grad_out, inner_out,
    own, peer, halo, halo_peer, src, edge_src, mid, edge_mid, grad, inner_curv,
    zmat, xmat, edge_xmat, ymat, zmat_wide, xmat_wide, edge_xmat_wide, ymat_wide,
    own_sem, matrix_sems, peer_sems, send_sems, recv_sems, corner_send, corner_recv, out_sems
):
    width = lines + SIDE
    group, me, core = lax.axis_index("groups"), lax.axis_index("gx"), lax.axis_index("gy")
    lower, upper = me > 0, me < count - 1
    load = pltpu.make_async_copy(level, own, own_sem)
    load.start()
    matrices = (
        (zmat_in, zmat_wide, zmat), (xmat_in, xmat_wide, xmat),
        (edge_xmat_in, edge_xmat_wide, edge_xmat), (ymat_in, ymat_wide, ymat))
    matrix_loads = [
        pltpu.make_async_copy(source, target, matrix_sems.at[number])
        for number, (source, target, _) in enumerate(matrices)]
    for copy in matrix_loads:
        copy.start()

    barrier = pltpu.get_barrier_semaphore()
    pl.semaphore_signal(barrier, inc=1, device_id=(group, me, 1 - core), device_id_type=MESH)

    @pl.when(lower)
    def _():
        pl.semaphore_signal(barrier, inc=1, device_id=(group, me - 1, core), device_id_type=MESH)

    @pl.when(upper)
    def _():
        pl.semaphore_signal(barrier, inc=1, device_id=(group, me + 1, core), device_id_type=MESH)

    pl.semaphore_wait(barrier, 1 + lower.astype(jnp.int32) + upper.astype(jnp.int32))

    def piece(number):
        offset, size = CHUNKS[number]
        start = jnp.where(core == 0, lines - offset - size, offset)
        return pl.multiple_of(start, 8), size

    near = pl.ds(piece(0)[0], SIDE)
    to_peer = pltpu.make_async_remote_copy(
        level.at[:, near], peer, peer_sems.at[0], peer_sems.at[1],
        device_id=(group, me, 1 - core), device_id_type=MESH)
    to_peer.start()

    def halo_copy(side, number):
        start, size = piece(number)
        cut = pl.ds(rows - REACH, REACH) if side == 0 else pl.ds(0, REACH)
        return pltpu.make_async_remote_copy(
            level.at[cut, pl.ds(start, size)], halo.at[side, :, pl.ds(start, size)],
            send_sems.at[side, number], recv_sems.at[side, number],
            device_id=(group, me + 1 if side == 0 else me - 1, core), device_id_type=MESH)

    for number in range(len(CHUNKS)):
        @pl.when(upper)
        def _():
            halo_copy(0, number).start()

        @pl.when(lower)
        def _():
            halo_copy(1, number).start()

    @pl.when(me == 0)
    def _():
        halo[0] = jnp.zeros((REACH, lines, 128), jnp.float32)
        halo_peer[0] = jnp.zeros((REACH, SIDE, 128), jnp.float32)

    @pl.when(me == count - 1)
    def _():
        halo[1] = jnp.zeros((REACH, lines, 128), jnp.float32)
        halo_peer[1] = jnp.zeros((REACH, SIDE, 128), jnp.float32)

    for side in range(2):
        edge_src[pl.ds((side * SIDE + REACH) * width, (SIDE - REACH) * width), :] = jnp.zeros(
            ((SIDE - REACH) * width, 128), jnp.float32)
    clear_pad(mid, out_rows, width)
    clear_pad(edge_mid, 2 * SIDE, width)

    for copy, (_, source, target) in zip(matrix_loads, matrices):
        copy.wait()
        target[...] = source[...].astype(jnp.bfloat16)
    load.wait()
    to_peer.wait()

    def place_own(x, carry):
        base = pl.multiple_of(x * width, 8)
        src[pl.ds(base, lines), :] = own[x]
        src[pl.ds(base + lines, SIDE), :] = peer[x]
        return carry

    lax.fori_loop(0, rows, place_own, 0)
    columns(src, rows, out_rows, zmat, xmat, mid, width, 0, width // 8)

    def own_plane(x, carry):
        for c, value in enumerate(plane(mid, ymat, core, x)):
            grad[c, x] = value
        return carry

    lax.fori_loop(0, rows + 2 * RIM, own_plane, 0, unroll=4)
    shift = rows + 2 * RIM - 2 * SIDE

    def inner_unit(x, carry):
        unit(grad, x)
        return carry

    lax.fori_loop(SIDE, SIDE + shift, inner_unit, 0, unroll=4)
    inner_rows = shift - 2 * RIM
    for first in range(SIDE, SIDE + inner_rows, 8):
        listed = listed_cells(band, me, core, first // BLOCK, rows, lines)

        def inner_divergence(x, carry):
            inner_curv[x - SIDE] = divergence(grad, x, lines) * listed
            return carry

        lax.fori_loop(first, first + 8, inner_divergence, 0, unroll=2)
    inner = pltpu.make_async_copy(
        grad.at[:, pl.ds(SIDE, shift)], grad_out.at[:, pl.ds(SIDE, shift)], out_sems.at[0])
    inner.start()
    inner_done = pltpu.make_async_copy(inner_curv, inner_out, out_sems.at[2 * SIDE // 8 + 1])
    inner_done.start()

    def corner(side):
        return pltpu.make_async_remote_copy(
            halo.at[side, :, near], halo_peer.at[side], corner_send.at[side], corner_recv.at[side],
            device_id=(group, me, 1 - core), device_id_type=MESH)

    def place_edge(ref, start, size, slot):
        def step(x, carry):
            for side in range(2):
                base = pl.multiple_of((side * SIDE + x) * width + slot, 8)
                edge_src[pl.ds(base, size), :] = ref[side, x, pl.ds(start, size), :]
            return carry

        lax.fori_loop(0, REACH, step, 0)

    def edge_columns(slot, size):
        columns(edge_src, 2 * SIDE, 2 * SIDE, zmat, edge_xmat, edge_mid, width, slot, size // 8)

    for number in range(len(CHUNKS)):
        start, size = piece(number)

        @pl.when(lower)
        def _():
            halo_copy(0, number).wait_recv()
            if number == 0:
                corner(0).start()

        @pl.when(upper)
        def _():
            halo_copy(1, number).wait_recv()
            if number == 0:
                corner(1).start()

        place_edge(halo, start, size, start)
        edge_columns(start, size)
        if number == 1:
            @pl.when(lower)
            def _():
                corner(0).wait()

            @pl.when(upper)
            def _():
                corner(1).wait()

            place_edge(halo_peer, 0, SIDE, lines)
            edge_columns(lines, SIDE)

    outs = [inner, inner_done]
    for number in range(2 * SIDE // 8):
        offset = 0 if number * 8 < SIDE else shift

        def edge_plane(x, carry):
            for c, value in enumerate(plane(edge_mid, ymat, core, x)):
                grad[c, x + offset] += value
            return carry

        lax.fori_loop(number * 8, number * 8 + 8, edge_plane, 0, unroll=4)
        done = pl.ds(number * 8 + offset, 8)
        outs.append(pltpu.make_async_copy(grad.at[:, done], grad_out.at[:, done], out_sems.at[number + 1]))
        outs[-1].start()
    for copy in outs:
        copy.wait()
    for number in range(len(CHUNKS)):
        @pl.when(upper)
        def _():
            halo_copy(0, number).wait_send()

        @pl.when(lower)
        def _():
            halo_copy(1, number).wait_send()


def normals_kernel(
    rows, lines, count, band, grad_in, inner_in, normals, curvature, grad, curv, in_sems, out_sems, inner_sems
):
    me, core = lax.axis_index("gx"), lax.axis_index("gy")
    mine = pl.ds(8, lines)
    inner_rows = rows - 2 * SIDE
    cut = SIDE + 2 * RIM
    spans = [(0, 12), (12, 8), (20, 8), (cut + inner_rows - 2 * RIM, 12), (cut + inner_rows + 8, 8),
             (cut + inner_rows + 16, 8)]
    loads = []
    for number, (first, size) in enumerate(spans):
        span = pl.ds(first, size)
        loads.append(pltpu.make_async_copy(grad_in.at[:, span], grad.at[:, span], in_sems.at[number]))
        loads[-1].start()
    span = pl.ds(cut, inner_rows - 2 * RIM)
    inner = pl.ds(SIDE, inner_rows)
    inner_loads = [
        pltpu.make_async_copy(grad_in.at[:, span], grad.at[:, span], inner_sems.at[0]),
        pltpu.make_async_copy(inner_in, curv.at[inner], inner_sems.at[1])]
    for copy in inner_loads:
        copy.start()
    outs = []

    def outside(first):
        for x in range(first, first + RIM):
            grad[0, x] = jnp.zeros((YOUT, 128), jnp.float32)

    starts = [0, 8, 16, rows - 24, rows - 16, rows - 8]
    for number, start in enumerate(starts):
        loads[number].wait()
        if number == 3:
            for copy in inner_loads:
                copy.wait()
            for c in range(3):
                outs.append(pltpu.make_async_copy(
                    grad.at[c, pl.ds(SIDE + RIM, inner_rows), mine], normals.at[c, inner], inner_sems.at[2 + c]))
                outs[-1].start()
            outs.append(pltpu.make_async_copy(curv.at[inner], curvature.at[inner], inner_sems.at[5]))
            outs[-1].start()
        first, size = spans[number]
        low = max(first, SIDE + inner_rows + 2 * RIM) if number >= 3 else first
        high = min(first + size, SIDE) if number < 3 else first + size

        def units(x, carry):
            unit(grad, x)
            return carry

        lax.fori_loop(low, high, units, 0, unroll=4)
        if number == 0:
            pl.when(me == 0)(functools.partial(outside, 0))
        if number == len(starts) - 1:
            pl.when(me == count - 1)(functools.partial(outside, rows + RIM))
        listed = listed_cells(band, me, core, start // BLOCK, rows, lines)

        def finish(x, carry):
            curv[x] = divergence(grad, x, lines) * listed
            return carry

        lax.fori_loop(start, start + 8, finish, 0, unroll=2)
        for c in range(3):
            outs.append(pltpu.make_async_copy(
                grad.at[c, pl.ds(start + RIM, 8), mine],
                normals.at[c, pl.ds(start, 8)], out_sems.at[number, c]))
            outs[-1].start()
        outs.append(pltpu.make_async_copy(
            curv.at[pl.ds(start, 8)], curvature.at[pl.ds(start, 8)], out_sems.at[number, 3]))
        outs[-1].start()
    for copy in outs:
        copy.wait()


def shards(level_set, band):
    rows, lines, depth = level_set.shape
    count = lax.axis_size("gx")
    width = lines + SIDE

    here = np.arange(depth)
    z_high, z_low = weight_halves(np.concatenate(weights(here, here, True), axis=0).T)
    zmat = np.concatenate([z_high, z_high, z_low], axis=0)

    def x_matrix(source, target):
        smooth, slope = weights(source, target, True)
        return np.concatenate([wide(slope), wide(smooth)], axis=0)

    out_rows = rows + 8
    far = -10000
    place = np.arange(2 * SIDE)
    edge_source = np.where(place < REACH, place - REACH, far)
    edge_source = np.where((place >= SIDE) & (place < SIDE + REACH), rows + place - SIDE, edge_source)
    edge_target = np.where(place < SIDE, place, place + rows + 2 * RIM - 2 * SIDE) - RIM
    xmat = x_matrix(np.arange(rows), np.arange(out_rows) - RIM)
    edge_xmat = x_matrix(edge_source, edge_target)

    slots = np.arange(YPAD)
    ymats = []
    for core in range(2):
        base = core * lines
        peer_base = lines if core == 0 else lines - SIDE
        source = np.where(slots < lines, base + slots, peer_base + slots - lines)
        source = np.where(slots < width, source, far)
        target = base - 8 + np.arange(YOUT)
        inside = ((target >= 0) & (target < 2 * lines))[:, None]
        ymats += [tall(values) for values in weights(source, target, inside)]
    ymat = np.stack(ymats)

    anywhere = pl.BlockSpec(memory_space=pl.ANY)
    smem = pl.BlockSpec(memory_space=pltpu.SMEM)
    blocks = jnp.transpose(band, (1, 2, 0))
    matrices = [matrix.astype(np.float32) for matrix in (zmat, xmat, edge_xmat, ymat)]
    inner_rows = rows - 2 * SIDE
    grad, inner = pl.pallas_call(
        functools.partial(gradient_kernel, rows, lines, out_rows, count),
        out_shape=(
            jax.ShapeDtypeStruct((3, out_rows, YOUT, depth), jnp.float32),
            jax.ShapeDtypeStruct((inner_rows, lines, depth), jnp.float32),
        ),
        in_specs=[anywhere, smem] + [anywhere] * 4,
        out_specs=(anywhere, anywhere),
        scratch_shapes=[
            pltpu.VMEM((rows, lines, depth), jnp.float32),
            pltpu.VMEM((rows, SIDE, depth), jnp.float32),
            pltpu.VMEM((2, REACH, lines, depth), jnp.float32),
            pltpu.VMEM((2, REACH, SIDE, depth), jnp.float32),
            pltpu.VMEM((rows * width, depth), jnp.float32),
            pltpu.VMEM((2 * SIDE * width, depth), jnp.float32),
            pltpu.VMEM((3, out_rows * YPAD, depth), jnp.float32),
            pltpu.VMEM((3, 2 * SIDE * YPAD, depth), jnp.float32),
            pltpu.VMEM((3, out_rows, YOUT, depth), jnp.float32),
            pltpu.VMEM((inner_rows, lines, depth), jnp.float32),
            *(pltpu.VMEM(matrix.shape, jnp.bfloat16) for matrix in matrices),
            *(pltpu.VMEM(matrix.shape, jnp.float32) for matrix in matrices),
            pltpu.SemaphoreType.DMA,
            pltpu.SemaphoreType.DMA((4,)),
            pltpu.SemaphoreType.DMA((2,)),
            pltpu.SemaphoreType.DMA((2, len(CHUNKS))),
            pltpu.SemaphoreType.DMA((2, len(CHUNKS))),
            pltpu.SemaphoreType.DMA((2,)),
            pltpu.SemaphoreType.DMA((2,)),
            pltpu.SemaphoreType.DMA((2 * SIDE // 8 + 2,)),
        ],
        compiler_params=pltpu.CompilerParams(
            vmem_limit_bytes=VMEM_BYTES, collective_id=0, has_side_effects=True),
        name="gradients",
    )(level_set, blocks, *(jnp.asarray(matrix) for matrix in matrices))
    return pl.pallas_call(
        functools.partial(normals_kernel, rows, lines, count),
        out_shape=(
            jax.ShapeDtypeStruct((3, rows, lines, depth), jnp.float32),
            jax.ShapeDtypeStruct((rows, lines, depth), jnp.float32),
        ),
        in_specs=[smem, anywhere, anywhere],
        out_specs=(anywhere, anywhere),
        scratch_shapes=[
            pltpu.VMEM((3, out_rows, YOUT, depth), jnp.float32),
            pltpu.VMEM((rows, lines, depth), jnp.float32),
            pltpu.SemaphoreType.DMA((6,)),
            pltpu.SemaphoreType.DMA((6, 4)),
            pltpu.SemaphoreType.DMA((6,)),
        ],
        compiler_params=pltpu.CompilerParams(vmem_limit_bytes=VMEM_BYTES),
        name="normals_and_divergence",
    )(blocks, grad, inner)


def solution(mesh):
    placed = (P(("groups", "gx"), "gy", None), P("groups", None, None))
    return jax.shard_map(
        shards,
        mesh=mesh,
        in_specs=placed,
        out_specs=(P(None, ("groups", "gx"), "gy", None), P(("groups", "gx"), "gy", None)),
        check_vma=False,
    )
```

```python
import functools

import jax
import jax.numpy as jnp
import ml_dtypes
import numpy as np
from jax import lax
from jax.experimental import pallas as pl
from jax.experimental.pallas import tpu as pltpu
from jax.sharding import PartitionSpec as P

HALF_TAPS = 20
BLOCK = 32
SIGMA_CELLS = 7.0
FLOOR_SQ = 0.05
RIM = 2
REACH = HALF_TAPS + RIM
SIDE = 24
YPAD = 96
YOUT = 80
VMEM_BYTES = 54 * 2**20
CHUNKS = ((0, 24), (24, 16), (40, 16), (56, 8))
MESH = pl.DeviceIdType.MESH


def weights(source, target, valid):
    offsets = np.arange(-HALF_TAPS, HALF_TAPS + 1).astype(np.float64)
    bell = np.exp(-offsets * offsets / (2.0 * SIGMA_CELLS * SIGMA_CELLS))
    total = np.sum(bell)
    moment = np.sum(offsets * offsets * (bell / total))
    distance = (source[None, :] - target[:, None]).astype(np.float64)
    inside = (np.abs(distance) <= HALF_TAPS) & valid
    values = np.exp(-np.where(inside, distance, 0.0) ** 2 / (2.0 * SIGMA_CELLS * SIGMA_CELLS)) / total
    values = np.where(inside, values, 0.0)
    return values, distance * values / moment


def weight_halves(values):
    high = values.astype(ml_dtypes.bfloat16)
    return high, (values - high.astype(np.float64)).astype(ml_dtypes.bfloat16)


def wide(values):
    high, low = weight_halves(values)
    return np.concatenate([high, high, low], axis=1)


def tall(values):
    high, low = weight_halves(values)
    return np.concatenate([np.concatenate([high, high], 1), np.concatenate([low, low], 1)], 0)


def halves(values):
    high = values.astype(jnp.bfloat16)
    low = (values - high.astype(jnp.float32)).astype(jnp.bfloat16)
    return high, low


def stack_halves(values):
    return jnp.concatenate(halves(values), axis=0)


def dot(a, b):
    return jnp.dot(a, b, preferred_element_type=jnp.float32)


def clear_pad(mid, planes, width):
    def clear(x, carry):
        for c in range(3):
            mid[c, pl.ds(pl.multiple_of(x * YPAD, 8) + width, YPAD - width), :] = jnp.zeros(
                (YPAD - width, 128), jnp.float32)
        return carry

    lax.fori_loop(0, planes, clear, 0)


def columns(src, rows, out_rows, zmat, xmat, mid, width, first, groups):
    def step(number, carry):
        base = first + number * 8
        lines = [src[pl.ds(base + i, rows, stride=width), :] for i in range(8)]
        high, low = halves(jnp.concatenate(lines, axis=0))
        along_z = dot(jnp.concatenate([high, low, high], axis=1), zmat[...])
        high, low = halves(along_z)
        for i in range(8):
            part = slice(i * rows, (i + 1) * rows)
            both = dot(xmat[...], jnp.concatenate([high[part], low[part], high[part]], axis=0))
            place = pl.ds(base + i, out_rows, stride=YPAD)
            mid[0, place, :] = both[:out_rows, :128]
            mid[1, place, :] = both[out_rows:, :128]
            mid[2, place, :] = both[out_rows:, 128:]
        return carry

    lax.fori_loop(0, groups, step, 0)


def plane(mid, ymat, core, x):
    place = pl.ds(pl.multiple_of(x * YPAD, 8), YPAD)
    first = stack_halves(mid[0, place, :])
    second = stack_halves(mid[1, place, :])
    third = stack_halves(mid[2, place, :])
    smooth = dot(ymat[2 * core], jnp.concatenate([first, third], axis=1))
    smooth = smooth[:YOUT] + smooth[YOUT:]
    slope = dot(ymat[2 * core + 1], second)
    return smooth[:, :128], slope[:YOUT] + slope[YOUT:], smooth[:, 128:]


def unit(grad, normal, x):
    first, second, third = grad[0, x], grad[1, x], grad[2, x]
    inverse = lax.rsqrt(jnp.maximum(first * first + second * second + third * third, FLOOR_SQ))
    normal[0, x] = first * inverse
    normal[1, x] = second * inverse
    normal[2, x] = third * inverse


def divergence(normal, x, lines):
    mine = pl.ds(8, lines)
    position = lax.broadcasted_iota(jnp.int32, (lines, 128), 1)
    total = normal[0, x, mine, :] - normal[0, x + 4, mine, :]
    total += normal[1, x + 2, pl.ds(6, lines), :] - normal[1, x + 2, pl.ds(10, lines), :]
    third = normal[2, x + 2, mine, :]
    total += jnp.where(position >= 2, pltpu.roll(third, 2, 1), 0.0)
    total -= jnp.where(position < 126, pltpu.roll(third, 126, 1), 0.0)
    near = normal[0, x + 3, mine, :] - normal[0, x + 1, mine, :]
    near += normal[1, x + 2, pl.ds(9, lines), :] - normal[1, x + 2, pl.ds(7, lines), :]
    near += jnp.where(position < 127, pltpu.roll(third, 127, 1), 0.0)
    near -= jnp.where(position >= 1, pltpu.roll(third, 1, 1), 0.0)
    return total + 8.0 * near


def listed_cells(band, me, core, block_x, rows, lines):
    lane = lax.broadcasted_iota(jnp.int32, (BLOCK, 128), 1)
    parts = []
    for block_y in range(lines // BLOCK):
        listed = jnp.zeros((BLOCK, 128), jnp.float32)
        for block_z in range(128 // BLOCK):
            value = band[core * (lines // BLOCK) + block_y, block_z, me * (rows // BLOCK) + block_x]
            listed = jnp.where(lane // BLOCK == block_z, value.astype(jnp.float32) * (1.0 / 12.0), listed)
        parts.append(listed)
    return jnp.concatenate(parts, axis=0)


def gradient_kernel(
    rows, lines, out_rows, count, level, band, zmat_in, xmat_in, edge_xmat_in, ymat_in, grad, inner_curv,
    own, peer, halo, halo_peer, src, edge_src, mid, edge_mid,
    zmat, xmat, edge_xmat, ymat, zmat_wide, xmat_wide, edge_xmat_wide, ymat_wide,
    own_sem, matrix_sems, peer_sems, send_sems, recv_sems, corner_send, corner_recv
):
    width = lines + SIDE
    group, me, core = lax.axis_index("groups"), lax.axis_index("gx"), lax.axis_index("gy")
    lower, upper = me > 0, me < count - 1
    load = pltpu.make_async_copy(level, own, own_sem)
    load.start()
    matrices = (
        (zmat_in, zmat_wide, zmat), (xmat_in, xmat_wide, xmat),
        (edge_xmat_in, edge_xmat_wide, edge_xmat), (ymat_in, ymat_wide, ymat))
    matrix_loads = [
        pltpu.make_async_copy(source, target, matrix_sems.at[number])
        for number, (source, target, _) in enumerate(matrices)]
    for copy in matrix_loads:
        copy.start()

    barrier = pltpu.get_barrier_semaphore()
    pl.semaphore_signal(barrier, inc=1, device_id=(group, me, 1 - core), device_id_type=MESH)

    @pl.when(lower)
    def _():
        pl.semaphore_signal(barrier, inc=1, device_id=(group, me - 1, core), device_id_type=MESH)

    @pl.when(upper)
    def _():
        pl.semaphore_signal(barrier, inc=1, device_id=(group, me + 1, core), device_id_type=MESH)

    pl.semaphore_wait(barrier, 1 + lower.astype(jnp.int32) + upper.astype(jnp.int32))

    def piece(number):
        offset, size = CHUNKS[number]
        start = jnp.where(core == 0, lines - offset - size, offset)
        return pl.multiple_of(start, 8), size

    near = pl.ds(piece(0)[0], SIDE)
    to_peer = pltpu.make_async_remote_copy(
        level.at[:, near], peer, peer_sems.at[0], peer_sems.at[1],
        device_id=(group, me, 1 - core), device_id_type=MESH)
    to_peer.start()

    def halo_copy(side, number):
        start, size = piece(number)
        cut = pl.ds(rows - REACH, REACH) if side == 0 else pl.ds(0, REACH)
        return pltpu.make_async_remote_copy(
            level.at[cut, pl.ds(start, size)], halo.at[side, :, pl.ds(start, size)],
            send_sems.at[side, number], recv_sems.at[side, number],
            device_id=(group, me + 1 if side == 0 else me - 1, core), device_id_type=MESH)

    for number in range(len(CHUNKS)):
        @pl.when(upper)
        def _():
            halo_copy(0, number).start()

        @pl.when(lower)
        def _():
            halo_copy(1, number).start()

    @pl.when(me == 0)
    def _():
        halo[0] = jnp.zeros((REACH, lines, 128), jnp.float32)
        halo_peer[0] = jnp.zeros((REACH, SIDE, 128), jnp.float32)

    @pl.when(me == count - 1)
    def _():
        halo[1] = jnp.zeros((REACH, lines, 128), jnp.float32)
        halo_peer[1] = jnp.zeros((REACH, SIDE, 128), jnp.float32)

    for side in range(2):
        edge_src[pl.ds((side * SIDE + REACH) * width, (SIDE - REACH) * width), :] = jnp.zeros(
            ((SIDE - REACH) * width, 128), jnp.float32)
    clear_pad(mid, out_rows, width)
    clear_pad(edge_mid, 2 * SIDE, width)

    for copy, (_, source, target) in zip(matrix_loads, matrices):
        copy.wait()
        target[...] = source[...].astype(jnp.bfloat16)
    load.wait()
    to_peer.wait()

    def place_own(x, carry):
        base = pl.multiple_of(x * width, 8)
        src[pl.ds(base, lines), :] = own[x]
        src[pl.ds(base + lines, SIDE), :] = peer[x]
        return carry

    lax.fori_loop(0, rows, place_own, 0)
    columns(src, rows, out_rows, zmat, xmat, mid, width, 0, width // 8)

    def own_plane(x, carry):
        for c, value in enumerate(plane(mid, ymat, core, x)):
            grad[c, x] = value
        return carry

    lax.fori_loop(0, rows + 2 * RIM, own_plane, 0, unroll=4)
    shift = rows + 2 * RIM - 2 * SIDE

    def inner_unit(x, carry):
        unit(grad, grad, x)
        return carry

    lax.fori_loop(SIDE, SIDE + shift, inner_unit, 0, unroll=4)
    inner_rows = shift - 2 * RIM
    for first in range(SIDE, SIDE + inner_rows, 8):
        listed = listed_cells(band, me, core, first // BLOCK, rows, lines)

        def inner_divergence(x, carry):
            inner_curv[x - SIDE] = divergence(grad, x, lines) * listed
            return carry

        lax.fori_loop(first, first + 8, inner_divergence, 0, unroll=2)

    def corner(side):
        return pltpu.make_async_remote_copy(
            halo.at[side, :, near], halo_peer.at[side], corner_send.at[side], corner_recv.at[side],
            device_id=(group, me, 1 - core), device_id_type=MESH)

    def place_edge(ref, start, size, slot):
        def step(x, carry):
            for side in range(2):
                base = pl.multiple_of((side * SIDE + x) * width + slot, 8)
                edge_src[pl.ds(base, size), :] = ref[side, x, pl.ds(start, size), :]
            return carry

        lax.fori_loop(0, REACH, step, 0)

    def edge_columns(slot, size):
        columns(edge_src, 2 * SIDE, 2 * SIDE, zmat, edge_xmat, edge_mid, width, slot, size // 8)

    for number in range(len(CHUNKS)):
        start, size = piece(number)

        @pl.when(lower)
        def _():
            halo_copy(0, number).wait_recv()
            if number == 0:
                corner(0).start()

        @pl.when(upper)
        def _():
            halo_copy(1, number).wait_recv()
            if number == 0:
                corner(1).start()

        place_edge(halo, start, size, start)
        edge_columns(start, size)
        if number == 1:
            @pl.when(lower)
            def _():
                corner(0).wait()

            @pl.when(upper)
            def _():
                corner(1).wait()

            place_edge(halo_peer, 0, SIDE, lines)
            edge_columns(lines, SIDE)

    def edge_planes(first, last, offset):
        def edge_plane(x, carry):
            for c, value in enumerate(plane(edge_mid, ymat, core, x)):
                grad[c, x + offset] += value
            return carry

        lax.fori_loop(first, last, edge_plane, 0, unroll=4)

    edge_planes(0, SIDE, 0)
    edge_planes(SIDE, 2 * SIDE, shift)
    for number in range(len(CHUNKS)):
        @pl.when(upper)
        def _():
            halo_copy(0, number).wait_send()

        @pl.when(lower)
        def _():
            halo_copy(1, number).wait_send()


def normals_kernel(rows, lines, count, band, grad, inner_curv, normals, curvature, normal, curv, sems, inner_sems):
    me, core = lax.axis_index("gx"), lax.axis_index("gy")
    mine = pl.ds(8, lines)
    inner_rows = rows - 2 * SIDE
    inner = pl.ds(SIDE, inner_rows)
    outs = []

    def send(source, target, sem):
        outs.append(pltpu.make_async_copy(source, target, sem))
        outs[-1].start()

    for c in range(3):
        send(grad.at[c, pl.ds(SIDE + RIM, inner_rows), mine], normals.at[c, inner], inner_sems.at[c])
    send(inner_curv, curvature.at[inner], inner_sems.at[3])

    def outside(first):
        for x in range(first, first + RIM):
            normal[0, x] = jnp.zeros((YOUT, 128), jnp.float32)

    def copy_plane(x, carry):
        for c in range(3):
            normal[c, x] = grad[c, x]
        return carry

    def units(first, size):
        def step(x, carry):
            unit(grad, normal, x)
            return carry

        lax.fori_loop(first, first + size, step, 0, unroll=4)

    for side in range(2):
        base = side * (rows - SIDE)
        ready = SIDE if side == 0 else SIDE + inner_rows
        lax.fori_loop(ready, ready + 2 * RIM, copy_plane, 0, unroll=4)
        for number in range(SIDE // 8):
            start = base + number * 8
            if side == 0:
                units(0 if number == 0 else start + 2 * RIM, (12, 8, 4)[number])
            else:
                units(start + 2 * RIM, 8)
            if start == 0:
                pl.when(me == 0)(functools.partial(outside, 0))
            if start == rows - 8:
                pl.when(me == count - 1)(functools.partial(outside, rows + RIM))
            listed = listed_cells(band, me, core, start // BLOCK, rows, lines)

            def finish(x, carry):
                curv[x] = divergence(normal, x, lines) * listed
                return carry

            lax.fori_loop(start, start + 8, finish, 0, unroll=2)
            place = side * (SIDE // 8) + number
            for c in range(3):
                send(normal.at[c, pl.ds(start + RIM, 8), mine], normals.at[c, pl.ds(start, 8)], sems.at[place, c])
            send(curv.at[pl.ds(start, 8)], curvature.at[pl.ds(start, 8)], sems.at[place, 3])
    for copy in outs:
        copy.wait()


def shards(level_set, band):
    rows, lines, depth = level_set.shape
    count = lax.axis_size("gx")
    width = lines + SIDE

    here = np.arange(depth)
    z_high, z_low = weight_halves(np.concatenate(weights(here, here, True), axis=0).T)
    zmat = np.concatenate([z_high, z_high, z_low], axis=0)

    def x_matrix(source, target):
        smooth, slope = weights(source, target, True)
        return np.concatenate([wide(slope), wide(smooth)], axis=0)

    out_rows = rows + 8
    far = -10000
    place = np.arange(2 * SIDE)
    edge_source = np.where(place < REACH, place - REACH, far)
    edge_source = np.where((place >= SIDE) & (place < SIDE + REACH), rows + place - SIDE, edge_source)
    edge_target = np.where(place < SIDE, place, place + rows + 2 * RIM - 2 * SIDE) - RIM
    xmat = x_matrix(np.arange(rows), np.arange(out_rows) - RIM)
    edge_xmat = x_matrix(edge_source, edge_target)

    slots = np.arange(YPAD)
    ymats = []
    for core in range(2):
        base = core * lines
        peer_base = lines if core == 0 else lines - SIDE
        source = np.where(slots < lines, base + slots, peer_base + slots - lines)
        source = np.where(slots < width, source, far)
        target = base - 8 + np.arange(YOUT)
        inside = ((target >= 0) & (target < 2 * lines))[:, None]
        ymats += [tall(values) for values in weights(source, target, inside)]
    ymat = np.stack(ymats)

    vmem, anywhere = pl.BlockSpec(memory_space=pltpu.VMEM), pl.BlockSpec(memory_space=pl.ANY)
    smem = pl.BlockSpec(memory_space=pltpu.SMEM)
    blocks = jnp.transpose(band, (1, 2, 0))
    matrices = [matrix.astype(np.float32) for matrix in (zmat, xmat, edge_xmat, ymat)]
    inner_rows = rows - 2 * SIDE
    grad, inner = pl.pallas_call(
        functools.partial(gradient_kernel, rows, lines, out_rows, count),
        out_shape=(
            pltpu.VMEM((3, out_rows, YOUT, depth), jnp.float32),
            pltpu.VMEM((inner_rows, lines, depth), jnp.float32),
        ),
        in_specs=[anywhere, smem] + [anywhere] * 4,
        out_specs=(vmem, vmem),
        scratch_shapes=[
            pltpu.VMEM((rows, lines, depth), jnp.float32),
            pltpu.VMEM((rows, SIDE, depth), jnp.float32),
            pltpu.VMEM((2, REACH, lines, depth), jnp.float32),
            pltpu.VMEM((2, REACH, SIDE, depth), jnp.float32),
            pltpu.VMEM((rows * width, depth), jnp.float32),
            pltpu.VMEM((2 * SIDE * width, depth), jnp.float32),
            pltpu.VMEM((3, out_rows * YPAD, depth), jnp.float32),
            pltpu.VMEM((3, 2 * SIDE * YPAD, depth), jnp.float32),
            *(pltpu.VMEM(matrix.shape, jnp.bfloat16) for matrix in matrices),
            *(pltpu.VMEM(matrix.shape, jnp.float32) for matrix in matrices),
            pltpu.SemaphoreType.DMA,
            pltpu.SemaphoreType.DMA((4,)),
            pltpu.SemaphoreType.DMA((2,)),
            pltpu.SemaphoreType.DMA((2, len(CHUNKS))),
            pltpu.SemaphoreType.DMA((2, len(CHUNKS))),
            pltpu.SemaphoreType.DMA((2,)),
            pltpu.SemaphoreType.DMA((2,)),
        ],
        compiler_params=pltpu.CompilerParams(
            vmem_limit_bytes=VMEM_BYTES, collective_id=0, has_side_effects=True),
        name="gradients",
    )(level_set, blocks, *(jnp.asarray(matrix) for matrix in matrices))
    return pl.pallas_call(
        functools.partial(normals_kernel, rows, lines, count),
        out_shape=(
            jax.ShapeDtypeStruct((3, rows, lines, depth), jnp.float32),
            jax.ShapeDtypeStruct((rows, lines, depth), jnp.float32),
        ),
        in_specs=[smem, vmem, vmem],
        out_specs=(anywhere, anywhere),
        scratch_shapes=[
            pltpu.VMEM((3, out_rows, YOUT, depth), jnp.float32),
            pltpu.VMEM((rows, lines, depth), jnp.float32),
            pltpu.SemaphoreType.DMA((6, 4)),
            pltpu.SemaphoreType.DMA((4,)),
        ],
        compiler_params=pltpu.CompilerParams(vmem_limit_bytes=24 * 2**20),
        name="normals_and_divergence",
    )(blocks, grad, inner)


def solution(mesh):
    placed = (P(("groups", "gx"), "gy", None), P("groups", None, None))
    return jax.shard_map(
        shards,
        mesh=mesh,
        in_specs=placed,
        out_specs=(P(None, ("groups", "gx"), "gy", None), P(("groups", "gx"), "gy", None)),
        check_vma=False,
    )
```

```python
import functools

import jax
import jax.numpy as jnp
import ml_dtypes
import numpy as np
from jax import lax
from jax.experimental import pallas as pl
from jax.experimental.pallas import tpu as pltpu
from jax.sharding import PartitionSpec as P

HALF_TAPS = 20
BLOCK = 32
SIGMA_CELLS = 7.0
FLOOR_SQ = 0.05
RIM = 2
REACH = HALF_TAPS + RIM
SIDE = 24
YPAD = 96
YOUT = 80
VMEM_BYTES = 54 * 2**20
CHUNKS = ((0, 16), (16, 16), (32, 16), (48, 16))
RELAYED = (3, 2, 1)
MESH = pl.DeviceIdType.MESH


def weights(source, target, valid):
    offsets = np.arange(-HALF_TAPS, HALF_TAPS + 1).astype(np.float64)
    bell = np.exp(-offsets * offsets / (2.0 * SIGMA_CELLS * SIGMA_CELLS))
    total = np.sum(bell)
    moment = np.sum(offsets * offsets * (bell / total))
    distance = (source[None, :] - target[:, None]).astype(np.float64)
    inside = (np.abs(distance) <= HALF_TAPS) & valid
    values = np.exp(-np.where(inside, distance, 0.0) ** 2 / (2.0 * SIGMA_CELLS * SIGMA_CELLS)) / total
    values = np.where(inside, values, 0.0)
    return values, distance * values / moment


def weight_halves(values):
    high = values.astype(ml_dtypes.bfloat16)
    return high, (values - high.astype(np.float64)).astype(ml_dtypes.bfloat16)


def wide(values):
    high, low = weight_halves(values)
    return np.concatenate([high, high, low], axis=1)


def tall(values):
    high, low = weight_halves(values)
    return np.concatenate([np.concatenate([high, high], 1), np.concatenate([low, low], 1)], 0)


def halves(values):
    high = values.astype(jnp.bfloat16)
    low = (values - high.astype(jnp.float32)).astype(jnp.bfloat16)
    return high, low


def stack_halves(values):
    return jnp.concatenate(halves(values), axis=0)


def dot(a, b):
    return jnp.dot(a, b, preferred_element_type=jnp.float32)


def clear_pad(mid, planes, width):
    def clear(x, carry):
        for c in range(3):
            mid[c, pl.ds(pl.multiple_of(x * YPAD, 8) + width, YPAD - width), :] = jnp.zeros(
                (YPAD - width, 128), jnp.float32)
        return carry

    lax.fori_loop(0, planes, clear, 0)


def columns(src, rows, out_rows, zmat, xmat, mid, width, first, groups):
    def step(number, carry):
        base = first + number * 8
        lines = [src[pl.ds(base + i, rows, stride=width), :] for i in range(8)]
        high, low = halves(jnp.concatenate(lines, axis=0))
        along_z = dot(jnp.concatenate([high, low, high], axis=1), zmat[...])
        high, low = halves(along_z)
        for i in range(8):
            part = slice(i * rows, (i + 1) * rows)
            both = dot(xmat[...], jnp.concatenate([high[part], low[part], high[part]], axis=0))
            place = pl.ds(base + i, out_rows, stride=YPAD)
            mid[0, place, :] = both[:out_rows, :128]
            mid[1, place, :] = both[out_rows:, :128]
            mid[2, place, :] = both[out_rows:, 128:]
        return carry

    lax.fori_loop(0, groups, step, 0)


def plane(mid, ymat, core, x):
    place = pl.ds(pl.multiple_of(x * YPAD, 8), YPAD)
    first = stack_halves(mid[0, place, :])
    second = stack_halves(mid[1, place, :])
    third = stack_halves(mid[2, place, :])
    smooth = dot(ymat[2 * core], jnp.concatenate([first, third], axis=1))
    smooth = smooth[:YOUT] + smooth[YOUT:]
    slope = dot(ymat[2 * core + 1], second)
    return smooth[:, :128], slope[:YOUT] + slope[YOUT:], smooth[:, 128:]


def unit(grad, normal, x):
    first, second, third = grad[0, x], grad[1, x], grad[2, x]
    inverse = lax.rsqrt(jnp.maximum(first * first + second * second + third * third, FLOOR_SQ))
    normal[0, x] = first * inverse
    normal[1, x] = second * inverse
    normal[2, x] = third * inverse


def divergence(normal, x, lines):
    mine = pl.ds(8, lines)
    position = lax.broadcasted_iota(jnp.int32, (lines, 128), 1)
    total = normal[0, x, mine, :] - normal[0, x + 4, mine, :]
    total += normal[1, x + 2, pl.ds(6, lines), :] - normal[1, x + 2, pl.ds(10, lines), :]
    third = normal[2, x + 2, mine, :]
    total += jnp.where(position >= 2, pltpu.roll(third, 2, 1), 0.0)
    total -= jnp.where(position < 126, pltpu.roll(third, 126, 1), 0.0)
    near = normal[0, x + 3, mine, :] - normal[0, x + 1, mine, :]
    near += normal[1, x + 2, pl.ds(9, lines), :] - normal[1, x + 2, pl.ds(7, lines), :]
    near += jnp.where(position < 127, pltpu.roll(third, 127, 1), 0.0)
    near -= jnp.where(position >= 1, pltpu.roll(third, 1, 1), 0.0)
    return total + 8.0 * near


def listed_cells(band, me, core, block_x, rows, lines):
    lane = lax.broadcasted_iota(jnp.int32, (BLOCK, 128), 1)
    parts = []
    for block_y in range(lines // BLOCK):
        listed = jnp.zeros((BLOCK, 128), jnp.float32)
        for block_z in range(128 // BLOCK):
            value = band[core * (lines // BLOCK) + block_y, block_z, me * (rows // BLOCK) + block_x]
            listed = jnp.where(lane // BLOCK == block_z, value.astype(jnp.float32) * (1.0 / 12.0), listed)
        parts.append(listed)
    return jnp.concatenate(parts, axis=0)


def gradient_kernel(
    rows, lines, out_rows, count, level, band, zmat_in, xmat_in, edge_xmat_in, ymat_in, grad, inner_curv,
    own, peer, halo, halo_peer, src, edge_src, mid, edge_mid,
    zmat, xmat, edge_xmat, ymat, zmat_wide, xmat_wide, edge_xmat_wide, ymat_wide,
    own_sem, matrix_sems, peer_sems, send_sems, recv_sems, corner_send, corner_recv,
    relay, relay_sends, relay_recvs, relay_outs
):
    width = lines + SIDE
    group, me, core = lax.axis_index("groups"), lax.axis_index("gx"), lax.axis_index("gy")
    lower, upper = me > 0, me < count - 1
    load = pltpu.make_async_copy(level, own, own_sem)
    load.start()
    matrices = (
        (zmat_in, zmat_wide, zmat), (xmat_in, xmat_wide, xmat),
        (edge_xmat_in, edge_xmat_wide, edge_xmat), (ymat_in, ymat_wide, ymat))
    matrix_loads = [
        pltpu.make_async_copy(source, target, matrix_sems.at[number])
        for number, (source, target, _) in enumerate(matrices)]
    for copy in matrix_loads:
        copy.start()

    barrier = pltpu.get_barrier_semaphore()
    pl.semaphore_signal(barrier, inc=1, device_id=(group, me, 1 - core), device_id_type=MESH)

    @pl.when(lower)
    def _():
        pl.semaphore_signal(barrier, inc=1, device_id=(group, me - 1, core), device_id_type=MESH)

    @pl.when(upper)
    def _():
        pl.semaphore_signal(barrier, inc=1, device_id=(group, me + 1, core), device_id_type=MESH)

    greeted = 1 + lower.astype(jnp.int32) + upper.astype(jnp.int32)
    relaying = count == 8
    if relaying:
        @pl.when(me >= 2)
        def _():
            pl.semaphore_signal(barrier, inc=1, device_id=(group, me - 2, core), device_id_type=MESH)

        @pl.when(me < count - 2)
        def _():
            pl.semaphore_signal(barrier, inc=1, device_id=(group, me + 2, core), device_id_type=MESH)

        greeted += (me >= 2).astype(jnp.int32) + (me < count - 2).astype(jnp.int32)
    pl.semaphore_wait(barrier, greeted)

    def piece(number):
        offset, size = CHUNKS[number]
        start = jnp.where(core == 0, lines - offset - size, offset)
        return pl.multiple_of(start, 8), size

    near = pl.ds(pl.multiple_of(jnp.where(core == 0, lines - SIDE, 0), 8), SIDE)
    to_peer = pltpu.make_async_remote_copy(
        level.at[:, near], peer, peer_sems.at[0], peer_sems.at[1],
        device_id=(group, me, 1 - core), device_id_type=MESH)
    to_peer.start()

    def halo_copy(side, number):
        start, size = piece(number)
        cut = pl.ds(rows - REACH, REACH) if side == 0 else pl.ds(0, REACH)
        return pltpu.make_async_remote_copy(
            level.at[cut, pl.ds(start, size)], halo.at[side, :, pl.ds(start, size)],
            send_sems.at[side, number], recv_sems.at[side, number],
            device_id=(group, me + 1 if side == 0 else me - 1, core), device_id_type=MESH)

    odd = me % 2 == 1
    sends_away = jnp.where(odd, me < count - 1, me >= 2)
    away = jnp.where(odd, 3 - (me - 1) // 2, me // 2)
    passes_on = jnp.where(odd, me >= 3, me < count - 2)
    passed = jnp.where(odd, (me - 1) // 2, 3 - me // 2)

    def detours(number, side):
        if not relaying or number not in RELAYED:
            return me < 0
        return sends_away & (odd if side == 0 else me % 2 == 0) & (number >= len(CHUNKS) - away)

    def to_relay(number):
        start, size = piece(number)
        cut = pl.ds(jnp.where(odd, rows - REACH, 0), REACH)
        return pltpu.make_async_remote_copy(
            level.at[cut, pl.ds(start, size)], relay.at[number],
            relay_sends.at[number], relay_recvs.at[number],
            device_id=(group, jnp.where(odd, me - 1, me + 1), core), device_id_type=MESH)

    def from_relay(number):
        start, size = piece(number)
        side = jnp.where(odd, 1, 0)
        return pltpu.make_async_remote_copy(
            relay.at[number], halo.at[side, :, pl.ds(start, size)],
            relay_outs.at[number], recv_sems.at[side, number],
            device_id=(group, jnp.where(odd, me - 2, me + 2), core), device_id_type=MESH)

    def relayed_here(number):
        return passes_on & (number >= len(CHUNKS) - passed)

    def pass_on(number):
        if relaying:
            @pl.when(relayed_here(number))
            def _():
                to_relay(number).wait_recv()
                from_relay(number).start()

    if relaying:
        for number in RELAYED:
            @pl.when(sends_away & (number >= len(CHUNKS) - away))
            def _():
                to_relay(number).start()

    for number in range(len(CHUNKS)):
        @pl.when(upper & jnp.logical_not(detours(number, 0)))
        def _():
            halo_copy(0, number).start()

        @pl.when(lower & jnp.logical_not(detours(number, 1)))
        def _():
            halo_copy(1, number).start()

    @pl.when(me == 0)
    def _():
        halo[0] = jnp.zeros((REACH, lines, 128), jnp.float32)
        halo_peer[0] = jnp.zeros((REACH, SIDE, 128), jnp.float32)

    @pl.when(me == count - 1)
    def _():
        halo[1] = jnp.zeros((REACH, lines, 128), jnp.float32)
        halo_peer[1] = jnp.zeros((REACH, SIDE, 128), jnp.float32)

    for side in range(2):
        edge_src[pl.ds((side * SIDE + REACH) * width, (SIDE - REACH) * width), :] = jnp.zeros(
            ((SIDE - REACH) * width, 128), jnp.float32)
    clear_pad(mid, out_rows, width)
    clear_pad(edge_mid, 2 * SIDE, width)

    for copy, (_, source, target) in zip(matrix_loads, matrices):
        copy.wait()
        target[...] = source[...].astype(jnp.bfloat16)
    load.wait()
    to_peer.wait()

    def place_own(x, carry):
        base = pl.multiple_of(x * width, 8)
        src[pl.ds(base, lines), :] = own[x]
        src[pl.ds(base + lines, SIDE), :] = peer[x]
        return carry

    lax.fori_loop(0, rows, place_own, 0)
    columns(src, rows, out_rows, zmat, xmat, mid, width, 0, width // 8)
    pass_on(3)

    def own_plane(x, carry):
        for c, value in enumerate(plane(mid, ymat, core, x)):
            grad[c, x] = value
        return carry

    lax.fori_loop(0, rows + 2 * RIM, own_plane, 0, unroll=4)
    pass_on(2)
    shift = rows + 2 * RIM - 2 * SIDE

    def inner_unit(x, carry):
        unit(grad, grad, x)
        return carry

    lax.fori_loop(SIDE, SIDE + shift, inner_unit, 0, unroll=4)
    inner_rows = shift - 2 * RIM
    for first in range(SIDE, SIDE + inner_rows, 8):
        listed = listed_cells(band, me, core, first // BLOCK, rows, lines)

        def inner_divergence(x, carry):
            inner_curv[x - SIDE] = divergence(grad, x, lines) * listed
            return carry

        lax.fori_loop(first, first + 8, inner_divergence, 0, unroll=2)

    pass_on(1)

    def corner(side):
        return pltpu.make_async_remote_copy(
            halo.at[side, :, near], halo_peer.at[side], corner_send.at[side], corner_recv.at[side],
            device_id=(group, me, 1 - core), device_id_type=MESH)

    def place_edge(ref, start, size, slot):
        def step(x, carry):
            for side in range(2):
                base = pl.multiple_of((side * SIDE + x) * width + slot, 8)
                edge_src[pl.ds(base, size), :] = ref[side, x, pl.ds(start, size), :]
            return carry

        lax.fori_loop(0, REACH, step, 0)

    def edge_columns(slot, size):
        columns(edge_src, 2 * SIDE, 2 * SIDE, zmat, edge_xmat, edge_mid, width, slot, size // 8)

    for number in range(len(CHUNKS)):
        start, size = piece(number)

        @pl.when(lower)
        def _():
            halo_copy(0, number).wait_recv()
            if number == 1:
                corner(0).start()

        @pl.when(upper)
        def _():
            halo_copy(1, number).wait_recv()
            if number == 1:
                corner(1).start()

        place_edge(halo, start, size, start)
        edge_columns(start, size)
        if number == 2:
            @pl.when(lower)
            def _():
                corner(0).wait()

            @pl.when(upper)
            def _():
                corner(1).wait()

            place_edge(halo_peer, 0, SIDE, lines)
            edge_columns(lines, SIDE)

    def edge_planes(first, last, offset):
        def edge_plane(x, carry):
            for c, value in enumerate(plane(edge_mid, ymat, core, x)):
                grad[c, x + offset] += value
            return carry

        lax.fori_loop(first, last, edge_plane, 0, unroll=4)

    edge_planes(0, SIDE, 0)
    edge_planes(SIDE, 2 * SIDE, shift)
    for number in range(len(CHUNKS)):
        @pl.when(upper & jnp.logical_not(detours(number, 0)))
        def _():
            halo_copy(0, number).wait_send()

        @pl.when(lower & jnp.logical_not(detours(number, 1)))
        def _():
            halo_copy(1, number).wait_send()

        if relaying and number in RELAYED:
            @pl.when(sends_away & (number >= len(CHUNKS) - away))
            def _():
                to_relay(number).wait_send()

            @pl.when(relayed_here(number))
            def _():
                from_relay(number).wait_send()


def normals_kernel(rows, lines, count, band, grad, inner_curv, normals, curvature, normal, curv, sems, inner_sems):
    me, core = lax.axis_index("gx"), lax.axis_index("gy")
    mine = pl.ds(8, lines)
    inner_rows = rows - 2 * SIDE
    inner = pl.ds(SIDE, inner_rows)
    outs = []

    def send(source, target, sem):
        outs.append(pltpu.make_async_copy(source, target, sem))
        outs[-1].start()

    for c in range(3):
        send(grad.at[c, pl.ds(SIDE + RIM, inner_rows), mine], normals.at[c, inner], inner_sems.at[c])
    send(inner_curv, curvature.at[inner], inner_sems.at[3])

    def outside(first):
        for x in range(first, first + RIM):
            normal[0, x] = jnp.zeros((YOUT, 128), jnp.float32)

    def copy_plane(x, carry):
        for c in range(3):
            normal[c, x] = grad[c, x]
        return carry

    def units(first, size):
        def step(x, carry):
            unit(grad, normal, x)
            return carry

        lax.fori_loop(first, first + size, step, 0, unroll=4)

    for side in range(2):
        base = side * (rows - SIDE)
        ready = SIDE if side == 0 else SIDE + inner_rows
        lax.fori_loop(ready, ready + 2 * RIM, copy_plane, 0, unroll=4)
        for number in range(SIDE // 8):
            start = base + number * 8
            if side == 0:
                units(0 if number == 0 else start + 2 * RIM, (12, 8, 4)[number])
            else:
                units(start + 2 * RIM, 8)
            if start == 0:
                pl.when(me == 0)(functools.partial(outside, 0))
            if start == rows - 8:
                pl.when(me == count - 1)(functools.partial(outside, rows + RIM))
            listed = listed_cells(band, me, core, start // BLOCK, rows, lines)

            def finish(x, carry):
                curv[x] = divergence(normal, x, lines) * listed
                return carry

            lax.fori_loop(start, start + 8, finish, 0, unroll=2)
            place = side * (SIDE // 8) + number
            for c in range(3):
                send(normal.at[c, pl.ds(start + RIM, 8), mine], normals.at[c, pl.ds(start, 8)], sems.at[place, c])
            send(curv.at[pl.ds(start, 8)], curvature.at[pl.ds(start, 8)], sems.at[place, 3])
    for copy in outs:
        copy.wait()


def shards(level_set, band):
    rows, lines, depth = level_set.shape
    count = lax.axis_size("gx")
    width = lines + SIDE

    here = np.arange(depth)
    z_high, z_low = weight_halves(np.concatenate(weights(here, here, True), axis=0).T)
    zmat = np.concatenate([z_high, z_high, z_low], axis=0)

    def x_matrix(source, target):
        smooth, slope = weights(source, target, True)
        return np.concatenate([wide(slope), wide(smooth)], axis=0)

    out_rows = rows + 8
    far = -10000
    place = np.arange(2 * SIDE)
    edge_source = np.where(place < REACH, place - REACH, far)
    edge_source = np.where((place >= SIDE) & (place < SIDE + REACH), rows + place - SIDE, edge_source)
    edge_target = np.where(place < SIDE, place, place + rows + 2 * RIM - 2 * SIDE) - RIM
    xmat = x_matrix(np.arange(rows), np.arange(out_rows) - RIM)
    edge_xmat = x_matrix(edge_source, edge_target)

    slots = np.arange(YPAD)
    ymats = []
    for core in range(2):
        base = core * lines
        peer_base = lines if core == 0 else lines - SIDE
        source = np.where(slots < lines, base + slots, peer_base + slots - lines)
        source = np.where(slots < width, source, far)
        target = base - 8 + np.arange(YOUT)
        inside = ((target >= 0) & (target < 2 * lines))[:, None]
        ymats += [tall(values) for values in weights(source, target, inside)]
    ymat = np.stack(ymats)

    vmem, anywhere = pl.BlockSpec(memory_space=pltpu.VMEM), pl.BlockSpec(memory_space=pl.ANY)
    smem = pl.BlockSpec(memory_space=pltpu.SMEM)
    blocks = jnp.transpose(band, (1, 2, 0))
    matrices = [matrix.astype(np.float32) for matrix in (zmat, xmat, edge_xmat, ymat)]
    inner_rows = rows - 2 * SIDE
    grad, inner = pl.pallas_call(
        functools.partial(gradient_kernel, rows, lines, out_rows, count),
        out_shape=(
            pltpu.VMEM((3, out_rows, YOUT, depth), jnp.float32),
            pltpu.VMEM((inner_rows, lines, depth), jnp.float32),
        ),
        in_specs=[anywhere, smem] + [anywhere] * 4,
        out_specs=(vmem, vmem),
        scratch_shapes=[
            pltpu.VMEM((rows, lines, depth), jnp.float32),
            pltpu.VMEM((rows, SIDE, depth), jnp.float32),
            pltpu.VMEM((2, REACH, lines, depth), jnp.float32),
            pltpu.VMEM((2, REACH, SIDE, depth), jnp.float32),
            pltpu.VMEM((rows * width, depth), jnp.float32),
            pltpu.VMEM((2 * SIDE * width, depth), jnp.float32),
            pltpu.VMEM((3, out_rows * YPAD, depth), jnp.float32),
            pltpu.VMEM((3, 2 * SIDE * YPAD, depth), jnp.float32),
            *(pltpu.VMEM(matrix.shape, jnp.bfloat16) for matrix in matrices),
            *(pltpu.VMEM(matrix.shape, jnp.float32) for matrix in matrices),
            pltpu.SemaphoreType.DMA,
            pltpu.SemaphoreType.DMA((4,)),
            pltpu.SemaphoreType.DMA((2,)),
            pltpu.SemaphoreType.DMA((2, len(CHUNKS))),
            pltpu.SemaphoreType.DMA((2, len(CHUNKS))),
            pltpu.SemaphoreType.DMA((2,)),
            pltpu.SemaphoreType.DMA((2,)),
            pltpu.VMEM((len(CHUNKS), REACH, CHUNKS[0][1], depth), jnp.float32),
            *(pltpu.SemaphoreType.DMA((len(CHUNKS),)) for _ in range(3)),
        ],
        compiler_params=pltpu.CompilerParams(
            vmem_limit_bytes=VMEM_BYTES, collective_id=0, has_side_effects=True),
        name="gradients",
    )(level_set, blocks, *(jnp.asarray(matrix) for matrix in matrices))
    return pl.pallas_call(
        functools.partial(normals_kernel, rows, lines, count),
        out_shape=(
            jax.ShapeDtypeStruct((3, rows, lines, depth), jnp.float32),
            jax.ShapeDtypeStruct((rows, lines, depth), jnp.float32),
        ),
        in_specs=[smem, vmem, vmem],
        out_specs=(anywhere, anywhere),
        scratch_shapes=[
            pltpu.VMEM((3, out_rows, YOUT, depth), jnp.float32),
            pltpu.VMEM((rows, lines, depth), jnp.float32),
            pltpu.SemaphoreType.DMA((6, 4)),
            pltpu.SemaphoreType.DMA((4,)),
        ],
        compiler_params=pltpu.CompilerParams(vmem_limit_bytes=24 * 2**20),
        name="normals_and_divergence",
    )(blocks, grad, inner)


def solution(mesh):
    placed = (P(("groups", "gx"), "gy", None), P("groups", None, None))
    return jax.shard_map(
        shards,
        mesh=mesh,
        in_specs=placed,
        out_specs=(P(None, ("groups", "gx"), "gy", None), P(("groups", "gx"), "gy", None)),
        check_vma=False,
    )
```

```python
import functools

import jax
import jax.numpy as jnp
import ml_dtypes
import numpy as np
from jax import lax
from jax.experimental import pallas as pl
from jax.experimental.pallas import tpu as pltpu
from jax.sharding import PartitionSpec as P

HALF_TAPS = 20
BLOCK = 32
SIGMA_CELLS = 7.0
FLOOR_SQ = 0.05
RIM = 2
REACH = HALF_TAPS + RIM
SIDE = 24
YPAD = 96
YOUT = 80
VMEM_BYTES = 54 * 2**20
CHUNKS = ((0, 16), (16, 16), (32, 16), (48, 16))
RELAYED = (1, 2, 3)
MESH = pl.DeviceIdType.MESH


def weights(source, target, valid):
    offsets = np.arange(-HALF_TAPS, HALF_TAPS + 1).astype(np.float64)
    bell = np.exp(-offsets * offsets / (2.0 * SIGMA_CELLS * SIGMA_CELLS))
    total = np.sum(bell)
    moment = np.sum(offsets * offsets * (bell / total))
    distance = (source[None, :] - target[:, None]).astype(np.float64)
    inside = (np.abs(distance) <= HALF_TAPS) & valid
    values = np.exp(-np.where(inside, distance, 0.0) ** 2 / (2.0 * SIGMA_CELLS * SIGMA_CELLS)) / total
    values = np.where(inside, values, 0.0)
    return values, distance * values / moment


def weight_halves(values):
    high = values.astype(ml_dtypes.bfloat16)
    return high, (values - high.astype(np.float64)).astype(ml_dtypes.bfloat16)


def wide(values):
    high, low = weight_halves(values)
    return np.concatenate([high, high, low], axis=1)


def tall(values):
    high, low = weight_halves(values)
    return np.concatenate([np.concatenate([high, high], 1), np.concatenate([low, low], 1)], 0)


def halves(values):
    high = values.astype(jnp.bfloat16)
    low = (values - high.astype(jnp.float32)).astype(jnp.bfloat16)
    return high, low


def stack_halves(values):
    return jnp.concatenate(halves(values), axis=0)


def dot(a, b):
    return jnp.dot(a, b, preferred_element_type=jnp.float32)


def clear_pad(mid, planes, width):
    def clear(x, carry):
        for c in range(3):
            mid[c, pl.ds(pl.multiple_of(x * YPAD, 8) + width, YPAD - width), :] = jnp.zeros(
                (YPAD - width, 128), jnp.float32)
        return carry

    lax.fori_loop(0, planes, clear, 0)


def columns(src, rows, out_rows, zmat, xmat, mid, width, first, groups):
    def step(number, carry):
        base = first + number * 8
        lines = [src[pl.ds(base + i, rows, stride=width), :] for i in range(8)]
        high, low = halves(jnp.concatenate(lines, axis=0))
        along_z = dot(jnp.concatenate([high, low, high], axis=1), zmat[...])
        high, low = halves(along_z)
        for i in range(8):
            part = slice(i * rows, (i + 1) * rows)
            both = dot(xmat[...], jnp.concatenate([high[part], low[part], high[part]], axis=0))
            place = pl.ds(base + i, out_rows, stride=YPAD)
            mid[0, place, :] = both[:out_rows, :128]
            mid[1, place, :] = both[out_rows:, :128]
            mid[2, place, :] = both[out_rows:, 128:]
        return carry

    lax.fori_loop(0, groups, step, 0)


def plane(parts, ymat, core):
    def field(c):
        return stack_halves(sum(mid[c, pl.ds(pl.multiple_of(x * YPAD, 8), YPAD), :] for mid, x in parts))

    first, second, third = field(0), field(1), field(2)
    smooth = dot(ymat[2 * core], jnp.concatenate([first, third], axis=1))
    smooth = smooth[:YOUT] + smooth[YOUT:]
    slope = dot(ymat[2 * core + 1], second)
    return smooth[:, :128], slope[:YOUT] + slope[YOUT:], smooth[:, 128:]


def unit(grad, normal, x):
    first, second, third = grad[0, x], grad[1, x], grad[2, x]
    inverse = lax.rsqrt(jnp.maximum(first * first + second * second + third * third, FLOOR_SQ))
    normal[0, x] = first * inverse
    normal[1, x] = second * inverse
    normal[2, x] = third * inverse


def divergence(normal, x, lines):
    mine = pl.ds(8, lines)
    position = lax.broadcasted_iota(jnp.int32, (lines, 128), 1)
    total = normal[0, x, mine, :] - normal[0, x + 4, mine, :]
    total += normal[1, x + 2, pl.ds(6, lines), :] - normal[1, x + 2, pl.ds(10, lines), :]
    third = normal[2, x + 2, mine, :]
    total += jnp.where(position >= 2, pltpu.roll(third, 2, 1), 0.0)
    total -= jnp.where(position < 126, pltpu.roll(third, 126, 1), 0.0)
    near = normal[0, x + 3, mine, :] - normal[0, x + 1, mine, :]
    near += normal[1, x + 2, pl.ds(9, lines), :] - normal[1, x + 2, pl.ds(7, lines), :]
    near += jnp.where(position < 127, pltpu.roll(third, 127, 1), 0.0)
    near -= jnp.where(position >= 1, pltpu.roll(third, 1, 1), 0.0)
    return total + 8.0 * near


def listed_cells(band, me, core, block_x, rows, lines):
    lane = lax.broadcasted_iota(jnp.int32, (BLOCK, 128), 1)
    parts = []
    for block_y in range(lines // BLOCK):
        listed = jnp.zeros((BLOCK, 128), jnp.float32)
        for block_z in range(128 // BLOCK):
            value = band[core * (lines // BLOCK) + block_y, block_z, me * (rows // BLOCK) + block_x]
            listed = jnp.where(lane // BLOCK == block_z, value.astype(jnp.float32) * (1.0 / 12.0), listed)
        parts.append(listed)
    return jnp.concatenate(parts, axis=0)


def gradient_kernel(
    rows, lines, out_rows, count, level, band, zmat_in, xmat_in, edge_xmat_in, ymat_in, grad, inner_curv,
    own, peer, halo, halo_peer, src, edge_src, mid, edge_mid,
    zmat, xmat, edge_xmat, ymat, zmat_wide, xmat_wide, edge_xmat_wide, ymat_wide,
    own_sem, matrix_sems, peer_sems, send_sems, recv_sems, corner_send, corner_recv,
    relay, relay_sends, relay_recvs, relay_outs
):
    width = lines + SIDE
    group, me, core = lax.axis_index("groups"), lax.axis_index("gx"), lax.axis_index("gy")
    lower, upper = me > 0, me < count - 1
    load = pltpu.make_async_copy(level, own, own_sem)
    load.start()
    matrices = (
        (zmat_in, zmat_wide, zmat), (xmat_in, xmat_wide, xmat),
        (edge_xmat_in, edge_xmat_wide, edge_xmat), (ymat_in, ymat_wide, ymat))
    matrix_loads = [
        pltpu.make_async_copy(source, target, matrix_sems.at[number])
        for number, (source, target, _) in enumerate(matrices)]
    for copy in matrix_loads:
        copy.start()

    barrier = pltpu.get_barrier_semaphore()
    pl.semaphore_signal(barrier, inc=1, device_id=(group, me, 1 - core), device_id_type=MESH)

    @pl.when(lower)
    def _():
        pl.semaphore_signal(barrier, inc=1, device_id=(group, me - 1, core), device_id_type=MESH)

    @pl.when(upper)
    def _():
        pl.semaphore_signal(barrier, inc=1, device_id=(group, me + 1, core), device_id_type=MESH)

    greeted = 1 + lower.astype(jnp.int32) + upper.astype(jnp.int32)
    relaying = count == 8
    if relaying:
        @pl.when(me >= 2)
        def _():
            pl.semaphore_signal(barrier, inc=1, device_id=(group, me - 2, core), device_id_type=MESH)

        @pl.when(me < count - 2)
        def _():
            pl.semaphore_signal(barrier, inc=1, device_id=(group, me + 2, core), device_id_type=MESH)

        greeted += (me >= 2).astype(jnp.int32) + (me < count - 2).astype(jnp.int32)
    pl.semaphore_wait(barrier, greeted)

    def piece(number):
        offset, size = CHUNKS[number]
        start = jnp.where(core == 0, lines - offset - size, offset)
        return pl.multiple_of(start, 8), size

    near = pl.ds(pl.multiple_of(jnp.where(core == 0, lines - SIDE, 0), 8), SIDE)
    to_peer = pltpu.make_async_remote_copy(
        level.at[:, near], peer, peer_sems.at[0], peer_sems.at[1],
        device_id=(group, me, 1 - core), device_id_type=MESH)
    to_peer.start()

    def halo_copy(side, number):
        start, size = piece(number)
        cut = pl.ds(rows - REACH, REACH) if side == 0 else pl.ds(0, REACH)
        return pltpu.make_async_remote_copy(
            level.at[cut, pl.ds(start, size)], halo.at[side, :, pl.ds(start, size)],
            send_sems.at[side, number], recv_sems.at[side, number],
            device_id=(group, me + 1 if side == 0 else me - 1, core), device_id_type=MESH)

    odd = me % 2 == 1
    sends_away = jnp.where(odd, me < count - 1, me >= 2)
    away = jnp.where(odd, 3 - (me - 1) // 2, me // 2)
    passes_on = jnp.where(odd, me >= 3, me < count - 2)
    passed = jnp.where(odd, (me - 1) // 2, 3 - me // 2)

    def detours(number, side):
        if not relaying or number not in RELAYED:
            return me < 0
        return sends_away & (odd if side == 0 else me % 2 == 0) & (number >= len(CHUNKS) - away)

    def to_relay(number):
        start, size = piece(number)
        cut = pl.ds(jnp.where(odd, rows - REACH, 0), REACH)
        return pltpu.make_async_remote_copy(
            level.at[cut, pl.ds(start, size)], relay.at[number],
            relay_sends.at[number], relay_recvs.at[number],
            device_id=(group, jnp.where(odd, me - 1, me + 1), core), device_id_type=MESH)

    def from_relay(number):
        start, size = piece(number)
        side = jnp.where(odd, 1, 0)
        return pltpu.make_async_remote_copy(
            relay.at[number], halo.at[side, :, pl.ds(start, size)],
            relay_outs.at[number], recv_sems.at[side, number],
            device_id=(group, jnp.where(odd, me - 2, me + 2), core), device_id_type=MESH)

    def relayed_here(number):
        return passes_on & (number >= len(CHUNKS) - passed)

    def pass_on(number):
        if relaying:
            @pl.when(relayed_here(number))
            def _():
                to_relay(number).wait_recv()
                from_relay(number).start()

    if relaying:
        for number in RELAYED:
            @pl.when(sends_away & (number >= len(CHUNKS) - away))
            def _():
                to_relay(number).start()

    for number in range(len(CHUNKS)):
        @pl.when(upper & jnp.logical_not(detours(number, 0)))
        def _():
            halo_copy(0, number).start()

        @pl.when(lower & jnp.logical_not(detours(number, 1)))
        def _():
            halo_copy(1, number).start()

    @pl.when(me == 0)
    def _():
        halo[0] = jnp.zeros((REACH, lines, 128), jnp.float32)
        halo_peer[0] = jnp.zeros((REACH, SIDE, 128), jnp.float32)

    @pl.when(me == count - 1)
    def _():
        halo[1] = jnp.zeros((REACH, lines, 128), jnp.float32)
        halo_peer[1] = jnp.zeros((REACH, SIDE, 128), jnp.float32)

    for side in range(2):
        edge_src[pl.ds((side * SIDE + REACH) * width, (SIDE - REACH) * width), :] = jnp.zeros(
            ((SIDE - REACH) * width, 128), jnp.float32)
    clear_pad(mid, out_rows, width)
    clear_pad(edge_mid, 2 * SIDE, width)

    for copy, (_, source, target) in zip(matrix_loads, matrices):
        copy.wait()
        target[...] = source[...].astype(jnp.bfloat16)
    load.wait()
    to_peer.wait()

    def place_own(x, carry):
        base = pl.multiple_of(x * width, 8)
        src[pl.ds(base, lines), :] = own[x]
        src[pl.ds(base + lines, SIDE), :] = peer[x]
        return carry

    lax.fori_loop(0, rows, place_own, 0)
    columns(src, rows, out_rows, zmat, xmat, mid, width, 0, width // 8)
    pass_on(1)

    def own_plane(x, carry):
        for c, value in enumerate(plane([(mid, x)], ymat, core)):
            grad[c, x] = value
        return carry

    shift = rows + 2 * RIM - 2 * SIDE
    lax.fori_loop(SIDE, SIDE + shift, own_plane, 0, unroll=4)

    pass_on(2)

    def inner_unit(x, carry):
        unit(grad, grad, x)
        return carry

    lax.fori_loop(SIDE, SIDE + shift, inner_unit, 0, unroll=4)
    inner_rows = shift - 2 * RIM
    for first in range(SIDE, SIDE + inner_rows, 8):
        listed = listed_cells(band, me, core, first // BLOCK, rows, lines)

        def inner_divergence(x, carry):
            inner_curv[x - SIDE] = divergence(grad, x, lines) * listed
            return carry

        lax.fori_loop(first, first + 8, inner_divergence, 0, unroll=2)

    pass_on(3)

    def corner(side):
        return pltpu.make_async_remote_copy(
            halo.at[side, :, near], halo_peer.at[side], corner_send.at[side], corner_recv.at[side],
            device_id=(group, me, 1 - core), device_id_type=MESH)

    def place_edge(ref, start, size, slot):
        def step(x, carry):
            for side in range(2):
                base = pl.multiple_of((side * SIDE + x) * width + slot, 8)
                edge_src[pl.ds(base, size), :] = ref[side, x, pl.ds(start, size), :]
            return carry

        lax.fori_loop(0, REACH, step, 0)

    def edge_columns(slot, size):
        columns(edge_src, 2 * SIDE, 2 * SIDE, zmat, edge_xmat, edge_mid, width, slot, size // 8)

    for number in range(len(CHUNKS)):
        start, size = piece(number)

        @pl.when(lower)
        def _():
            halo_copy(0, number).wait_recv()
            if number == 1:
                corner(0).start()

        @pl.when(upper)
        def _():
            halo_copy(1, number).wait_recv()
            if number == 1:
                corner(1).start()

        place_edge(halo, start, size, start)
        edge_columns(start, size)
        if number == 2:
            @pl.when(lower)
            def _():
                corner(0).wait()

            @pl.when(upper)
            def _():
                corner(1).wait()

            place_edge(halo_peer, 0, SIDE, lines)
            edge_columns(lines, SIDE)

    def edge_planes(first, last, offset):
        def edge_plane(x, carry):
            for c, value in enumerate(plane([(mid, x + offset), (edge_mid, x)], ymat, core)):
                grad[c, x + offset] = value
            return carry

        lax.fori_loop(first, last, edge_plane, 0, unroll=4)

    edge_planes(0, SIDE, 0)
    edge_planes(SIDE, 2 * SIDE, shift)
    for number in range(len(CHUNKS)):
        @pl.when(upper & jnp.logical_not(detours(number, 0)))
        def _():
            halo_copy(0, number).wait_send()

        @pl.when(lower & jnp.logical_not(detours(number, 1)))
        def _():
            halo_copy(1, number).wait_send()

        if relaying and number in RELAYED:
            @pl.when(sends_away & (number >= len(CHUNKS) - away))
            def _():
                to_relay(number).wait_send()

            @pl.when(relayed_here(number))
            def _():
                from_relay(number).wait_send()


def normals_kernel(rows, lines, count, band, grad, inner_curv, normals, curvature, normal, curv, sems, inner_sems):
    me, core = lax.axis_index("gx"), lax.axis_index("gy")
    mine = pl.ds(8, lines)
    inner_rows = rows - 2 * SIDE
    inner = pl.ds(SIDE, inner_rows)
    outs = []

    def send(source, target, sem):
        outs.append(pltpu.make_async_copy(source, target, sem))
        outs[-1].start()

    for c in range(3):
        send(grad.at[c, pl.ds(SIDE + RIM, inner_rows), mine], normals.at[c, inner], inner_sems.at[c])
    send(inner_curv, curvature.at[inner], inner_sems.at[3])

    def outside(first):
        for x in range(first, first + RIM):
            normal[0, x] = jnp.zeros((YOUT, 128), jnp.float32)

    def copy_plane(x, carry):
        for c in range(3):
            normal[c, x] = grad[c, x]
        return carry

    def units(first, size):
        def step(x, carry):
            unit(grad, normal, x)
            return carry

        lax.fori_loop(first, first + size, step, 0, unroll=4)

    for side in range(2):
        base = side * (rows - SIDE)
        ready = SIDE if side == 0 else SIDE + inner_rows
        lax.fori_loop(ready, ready + 2 * RIM, copy_plane, 0, unroll=4)
        for number in range(SIDE // 8):
            start = base + number * 8
            if side == 0:
                units(0 if number == 0 else start + 2 * RIM, (12, 8, 4)[number])
            else:
                units(start + 2 * RIM, 8)
            if start == 0:
                pl.when(me == 0)(functools.partial(outside, 0))
            if start == rows - 8:
                pl.when(me == count - 1)(functools.partial(outside, rows + RIM))
            listed = listed_cells(band, me, core, start // BLOCK, rows, lines)

            def finish(x, carry):
                curv[x] = divergence(normal, x, lines) * listed
                return carry

            lax.fori_loop(start, start + 8, finish, 0, unroll=2)
            place = side * (SIDE // 8) + number
            for c in range(3):
                send(normal.at[c, pl.ds(start + RIM, 8), mine], normals.at[c, pl.ds(start, 8)], sems.at[place, c])
            send(curv.at[pl.ds(start, 8)], curvature.at[pl.ds(start, 8)], sems.at[place, 3])
    for copy in outs:
        copy.wait()


def shards(level_set, band):
    rows, lines, depth = level_set.shape
    count = lax.axis_size("gx")
    width = lines + SIDE

    here = np.arange(depth)
    z_high, z_low = weight_halves(np.concatenate(weights(here, here, True), axis=0).T)
    zmat = np.concatenate([z_high, z_high, z_low], axis=0)

    def x_matrix(source, target):
        smooth, slope = weights(source, target, True)
        return np.concatenate([wide(slope), wide(smooth)], axis=0)

    out_rows = rows + 8
    far = -10000
    place = np.arange(2 * SIDE)
    edge_source = np.where(place < REACH, place - REACH, far)
    edge_source = np.where((place >= SIDE) & (place < SIDE + REACH), rows + place - SIDE, edge_source)
    edge_target = np.where(place < SIDE, place, place + rows + 2 * RIM - 2 * SIDE) - RIM
    xmat = x_matrix(np.arange(rows), np.arange(out_rows) - RIM)
    edge_xmat = x_matrix(edge_source, edge_target)

    slots = np.arange(YPAD)
    ymats = []
    for core in range(2):
        base = core * lines
        peer_base = lines if core == 0 else lines - SIDE
        source = np.where(slots < lines, base + slots, peer_base + slots - lines)
        source = np.where(slots < width, source, far)
        target = base - 8 + np.arange(YOUT)
        inside = ((target >= 0) & (target < 2 * lines))[:, None]
        ymats += [tall(values) for values in weights(source, target, inside)]
    ymat = np.stack(ymats)

    vmem, anywhere = pl.BlockSpec(memory_space=pltpu.VMEM), pl.BlockSpec(memory_space=pl.ANY)
    smem = pl.BlockSpec(memory_space=pltpu.SMEM)
    blocks = jnp.transpose(band, (1, 2, 0))
    matrices = [matrix.astype(np.float32) for matrix in (zmat, xmat, edge_xmat, ymat)]
    inner_rows = rows - 2 * SIDE
    grad, inner = pl.pallas_call(
        functools.partial(gradient_kernel, rows, lines, out_rows, count),
        out_shape=(
            pltpu.VMEM((3, out_rows, YOUT, depth), jnp.float32),
            pltpu.VMEM((inner_rows, lines, depth), jnp.float32),
        ),
        in_specs=[anywhere, smem] + [anywhere] * 4,
        out_specs=(vmem, vmem),
        scratch_shapes=[
            pltpu.VMEM((rows, lines, depth), jnp.float32),
            pltpu.VMEM((rows, SIDE, depth), jnp.float32),
            pltpu.VMEM((2, REACH, lines, depth), jnp.float32),
            pltpu.VMEM((2, REACH, SIDE, depth), jnp.float32),
            pltpu.VMEM((rows * width, depth), jnp.float32),
            pltpu.VMEM((2 * SIDE * width, depth), jnp.float32),
            pltpu.VMEM((3, out_rows * YPAD, depth), jnp.float32),
            pltpu.VMEM((3, 2 * SIDE * YPAD, depth), jnp.float32),
            *(pltpu.VMEM(matrix.shape, jnp.bfloat16) for matrix in matrices),
            *(pltpu.VMEM(matrix.shape, jnp.float32) for matrix in matrices),
            pltpu.SemaphoreType.DMA,
            pltpu.SemaphoreType.DMA((4,)),
            pltpu.SemaphoreType.DMA((2,)),
            pltpu.SemaphoreType.DMA((2, len(CHUNKS))),
            pltpu.SemaphoreType.DMA((2, len(CHUNKS))),
            pltpu.SemaphoreType.DMA((2,)),
            pltpu.SemaphoreType.DMA((2,)),
            pltpu.VMEM((len(CHUNKS), REACH, CHUNKS[0][1], depth), jnp.float32),
            *(pltpu.SemaphoreType.DMA((len(CHUNKS),)) for _ in range(3)),
        ],
        compiler_params=pltpu.CompilerParams(
            vmem_limit_bytes=VMEM_BYTES, collective_id=0, has_side_effects=True),
        name="gradients",
    )(level_set, blocks, *(jnp.asarray(matrix) for matrix in matrices))
    return pl.pallas_call(
        functools.partial(normals_kernel, rows, lines, count),
        out_shape=(
            jax.ShapeDtypeStruct((3, rows, lines, depth), jnp.float32),
            jax.ShapeDtypeStruct((rows, lines, depth), jnp.float32),
        ),
        in_specs=[smem, vmem, vmem],
        out_specs=(anywhere, anywhere),
        scratch_shapes=[
            pltpu.VMEM((3, out_rows, YOUT, depth), jnp.float32),
            pltpu.VMEM((rows, lines, depth), jnp.float32),
            pltpu.SemaphoreType.DMA((6, 4)),
            pltpu.SemaphoreType.DMA((4,)),
        ],
        compiler_params=pltpu.CompilerParams(vmem_limit_bytes=24 * 2**20),
        name="normals_and_divergence",
    )(blocks, grad, inner)


def solution(mesh):
    placed = (P(("groups", "gx"), "gy", None), P("groups", None, None))
    return jax.shard_map(
        shards,
        mesh=mesh,
        in_specs=placed,
        out_specs=(P(None, ("groups", "gx"), "gy", None), P(("groups", "gx"), "gy", None)),
        check_vma=False,
    )
```
